256 devices in a mesh: dp: 2 (over core), seq: 4 (over x), head: 32 (over z, y).
Axes of the slice: x: 4, y: 4, z: 8, core: 2. Of those that a mesh axis runs over, the one named last changes fastest.
Arguments:
- tokens_in: bfloat16 [32768, 3072], P(('dp', 'head'), 'seq'), parts along dimension 0, may hold values from -6 to 6
- qkv_weight: bfloat16 [3072, 3, 1536], P('head', None, 'seq'), may hold values from -0.109375 to 0.109375
- norm_gains: float32 [2, 128], replicated, may hold values from 0.1 to 1.9
- out_weight: bfloat16 [3072, 1536], P('seq', 'head'), may hold values from -0.15625 to 0.15625
- neighbours: int32 [256, 10], P(('dp', 'head')), parts along dimension 0, may hold values from -1 to 127, as said below
Outputs:
- attended: bfloat16 [32768, 3072], P(('dp', 'head'), 'seq'), parts along dimension 0
The draws below stay inside these ranges and needn't reach their ends.
There are 2 independent parts, one for each index of `dp`. The reference program is written for one: setup_inputs(seed, part) draws one part's arguments, and reference() takes and returns one part's arrays. A program takes and returns all parts, laid end to end along the dimension named above; an argument that names none is the same for every part. Nothing has to cross between parts.
Inputs may be any that keep to these rules, and one draw needn't show every extreme that they name: `neighbours`: tiles are numbered in raster order over a clip of 32 x 2 x 2 tiles. Slot 0 of row t is t itself; the other slots name distinct tiles other than t that lie within one tile of t along each of the three dimensions, or -1, in no particular order.
All inputs are finite; a program needn't handle non-finite values.
Results may differ from the reference program's by a relative error of at most 0.008.
Values may be sent and summed in bfloat16 or wider, within the bound.
No kernel may reach another device: no remote copies, remote signals or barrier semaphores. Data moves between devices by JAX's collectives and lax.ppermute only.
A program may use at most 64 MiB of HBM per device.

```python
import jax
import jax.numpy as jnp
from jax import lax

D = 3072
HD = 128
TILE = 128
HT = 2
WT = 2
WIN = 10
HEADS = 12
NTILES = 128
TOKENS = 16384


def draw_neighbours(key, part):
    key = jax.random.fold_in(key, 11)
    offsets = [(a, b, c) for a in (-1, 0, 1) for b in (-1, 0, 1) for c in (-1, 0, 1) if (a, b, c) != (0, 0, 0)]
    table = jnp.array(offsets, dtype=jnp.int32)
    frames = NTILES // (HT * WT)
    tiles = jnp.arange(NTILES, dtype=jnp.int32)
    frame = tiles // (HT * WT)
    row = tiles // WT % HT
    column = tiles % WT
    near_frame = frame[:, None] + table[None, :, 0]
    near_row = row[:, None] + table[None, :, 1]
    near_column = column[:, None] + table[None, :, 2]
    inside = (near_frame >= 0) & (near_frame < frames) & (near_row >= 0) & (near_row < HT) & (near_column >= 0) & (near_column < WT)
    target = near_frame * (HT * WT) + near_row * WT + near_column
    count = table.shape[0]
    ranks = jnp.arange(count, dtype=jnp.int32)
    priority = jax.random.randint(key, (NTILES, count), 0, 1 << 20, dtype=jnp.int32) * 32 + ranks[None, :]
    priority = jnp.where(inside, priority, -1 - ranks[None, :])
    best, where_best = lax.top_k(priority, WIN - 1)
    chosen = jnp.take_along_axis(target, where_best, axis=1)
    chosen = jnp.where(best >= 0, chosen, -1)
    return jnp.concatenate([tiles[:, None], chosen], axis=1).astype(jnp.int32)


def block_levels(own_key, shape, shards, smallest, high):
    level, own = 1.0, jax.random.fold_in(own_key, 6)
    for axis_at, parts in shards:
        heights = jnp.exp(jax.random.uniform(jax.random.fold_in(own, axis_at), (parts,), jnp.float32, smallest / len(shards), high / len(shards)))
        level = level * jnp.repeat(heights, shape[axis_at] // parts).reshape([-1 if axis == axis_at else 1 for axis in range(len(shape))])
    return level


def normal_values(rng, dims, width, bound, shards=(), kind=jnp.bfloat16):
    drawn = width * jax.random.normal(rng, dims, jnp.float32)
    if shards:
        drawn = drawn * block_levels(rng, dims, shards, -0.22, 0.18)
    return jnp.clip(drawn, -bound, bound).astype(kind)


def setup_inputs(seed: int = 0, part: int = 0) -> dict:
    streams_of = jax.random.split(jax.random.key(seed), 6)
    part_splits = jax.random.split(jax.random.fold_in(streams_of[5], part), 6)
    return {
        "tokens_in": normal_values(part_splits[0], (TOKENS, D), 1.0, 6.0, ((0, 32), (1, 4))),
        "qkv_weight": normal_values(streams_of[1], (D, 3, HEADS * HD), D ** -0.5, 0.109375, ((0, 32), (2, 4))),
        "norm_gains": jnp.clip(1.0 + 0.18 * jax.random.normal(streams_of[2], (2, HD), jnp.float32), 0.1, 1.9),
        "out_weight": normal_values(streams_of[3], (D, HEADS * HD), (HEADS * HD) ** -0.5, 0.15625, ((0, 4), (1, 32))),
        "neighbours": draw_neighbours(jax.random.fold_in(jax.random.fold_in(streams_of[5], part), 71), part),
    }


def rms_normed(values, gain):
    mean_sq = lax.optimization_barrier(jnp.mean(values * values, axis=-1, keepdims=True))
    return values * lax.rsqrt(mean_sq + 1e-06) * gain

def reference(tokens_in, qkv_weight, norm_gains, out_weight, neighbours):
    projected = jnp.dot(tokens_in, qkv_weight.reshape(D, 3 * HEADS * HD), preferred_element_type=jnp.float32)
    projected = projected.reshape(TOKENS, 3, HEADS, HD)
    query_normed = rms_normed(projected[:, 0], norm_gains[0]).astype(jnp.bfloat16)
    key_normed = rms_normed(projected[:, 1], norm_gains[1]).astype(jnp.bfloat16)
    value_rounded = projected[:, 2].astype(jnp.bfloat16)
    key_tiles = key_normed.reshape(NTILES, TILE, HEADS, HD)
    value_tiles = value_rounded.reshape(NTILES, TILE, HEADS, HD)
    query_tiles = query_normed.reshape(NTILES, TILE, HEADS, HD)
    scale = HD ** (-0.5)

    def one_tile(items):
        query_tile, listed = items
        usable = listed >= 0
        picked = jnp.maximum(listed, 0).astype(jnp.int32)
        keys = key_tiles[picked].reshape(WIN * TILE, HEADS, HD).astype(jnp.float32)
        values = value_tiles[picked].reshape(WIN * TILE, HEADS, HD).astype(jnp.float32)
        score = jnp.einsum('qhd,khd->hqk', query_tile.astype(jnp.float32), keys) * scale
        keep = jnp.repeat(usable, TILE)
        weight_exp = jnp.where(keep[None, None, :], jnp.exp(score), 0.0).astype(jnp.bfloat16)
        wide = weight_exp.astype(jnp.float32)
        numer = jnp.einsum('hqk,khd->qhd', wide, values)
        denom = lax.optimization_barrier(jnp.sum(wide, axis=-1))
        return (numer / jnp.transpose(denom)[:, :, None]).astype(jnp.bfloat16)
    head_out = lax.map(one_tile, (query_tiles, neighbours)).reshape(TOKENS, HEADS * HD)
    attended = jnp.dot(head_out, jnp.transpose(out_weight), preferred_element_type=jnp.float32)
    return attended.astype(jnp.bfloat16)
```

```python
import functools
import math

import jax
import jax.numpy as jnp
from jax import lax
from jax.experimental import pallas as pl
from jax.experimental.pallas import tpu as pltpu
from jax.sharding import PartitionSpec as P

HD = 128
TILE = 128
FRAME = 4
NY, NZ = 4, 8
BF = jnp.bfloat16
ANY = pl.BlockSpec(memory_space=pl.ANY)
VMEM = pl.BlockSpec(memory_space=pltpu.VMEM)
SMEM = pl.BlockSpec(memory_space=pltpu.SMEM)
LIMIT = 48 * 1024 * 1024

Y_FIRST_SUB = (0, -1, 1, 2)
Z_FIRST_SUB = (0, -2, 2, 4)
Y_FIRST_BUF = (0, -1, 1, -2, 2, -3, 3, -4)
Z_FIRST_BUF = ((0, 0), (1, 0), (0, 1), (1, -1), (0, 2), (1, -2), (0, 3), (1, -3))


def moved(x, core0, core1):
    pairs = []
    for core, (dz, dy) in enumerate((core0, core1)):
        for z in range(NZ):
            for y in range(NY):
                target = ((z + dz) % NZ) * NY + (y + dy) % NY
                pairs.append((core * NZ * NY + z * NY + y, core * NZ * NY + target))
    return lax.ppermute(x, ("dp", "head"), pairs)


def along(x, axis, step):
    n = lax.axis_size(axis)
    return lax.ppermute(x, axis, [(i, (i + step) % n) for i in range(n)])


def swapped(x):
    return lax.ppermute(x, "dp", [(0, 1), (1, 0)])


def ring_x(x):
    half = x.shape[0] // 2
    below = along(x, "seq", 1)
    above = along(x, "seq", -1)
    far_top = along(below[:half], "seq", 1)
    far_bottom = along(above[half:], "seq", -1)
    return below, above, far_top, far_bottom


def weight_buffers(mine):
    a = moved(mine, (0, 1), (2, 0))
    b = moved(mine, (0, -1), (-2, 0))
    c = moved(mine, (0, 2), (4, 0))
    start = jnp.concatenate([mine, a, b, c], axis=1)
    p1 = moved(start, (1, 0), (-1, 0))
    p2 = moved(start, (-1, 0), (0, -1))
    p3 = moved(p1, (1, 0), (0, 1))
    p4 = moved(p2, (-1, 0), (0, -1))
    p5 = moved(p3, (1, 0), (0, 1))
    p6 = moved(p4, (-1, 0), (0, -1))
    p7 = moved(p5, (1, 0), (0, 1))
    return [start, p1, p2, p3, p4, p5, p6, p7]


def row_table(z, y, core, rows):
    table = []
    for k in range(8):
        for i in range(4):
            z0, y0 = (z + Y_FIRST_BUF[k]) % NZ, (y + Y_FIRST_SUB[i]) % NY
            z1 = (z + Z_FIRST_BUF[k][0] + Z_FIRST_SUB[i]) % NZ
            y1 = (y + Z_FIRST_BUF[k][1]) % NY
            block = jnp.where(core == 0, z0 * NY + y0, z1 * NY + y1)
            table.append((block * 2 + core) * rows)
    return table


def normed(values, gain):
    mean_sq = jnp.mean(values * values, axis=-1, keepdims=True)
    return (values * lax.rsqrt(mean_sq + 1e-06) * gain).astype(BF)


def project_kernel(rows, place, token_place, *refs):
    gains = refs[0]
    tokens = refs[1:6]
    weights = refs[6:22]
    q_ref, kv_ref = refs[22:24]
    x, w, x_sem, w_sem = refs[24:]
    feats = tokens[0].shape[1]
    half = tokens[3].shape[0]
    copies = []
    starts = (0, 0, 0, 0, half)
    for i, ref in enumerate(tokens):
        n = ref.shape[0]
        at = pl.multiple_of(token_place[i], 128)
        copies.append(
            pltpu.make_async_copy(ref, x.at[pl.ds(starts[i], n), pl.ds(at, feats)], x_sem.at[i])
        )
    for k, ref in enumerate(weights):
        for i in range(4):
            at = pl.multiple_of(place[k * 4 + i], 16)
            copies.append(
                pltpu.make_async_copy(
                    ref.at[:, pl.ds(i * rows, rows), :], w.at[:, pl.ds(at, rows), :], w_sem.at[k, i]
                )
            )
    for c in copies:
        c.start()
    for c in copies:
        c.wait()
    heads = q_ref.shape[1] // HD
    for j in range(3):
        out = jnp.dot(x[...], w[j], preferred_element_type=jnp.float32)
        for h in range(heads):
            part = out[:, h * HD : (h + 1) * HD]
            if j == 0:
                q_ref[:, h * HD : (h + 1) * HD] = normed(part, gains[0:1, :])
            elif j == 1:
                kv_ref[:, h * HD : (h + 1) * HD] = normed(part, gains[1:2, :])
            else:
                at = (heads + h) * HD
                kv_ref[:, at : at + HD] = part.astype(BF)


def project(place, token_place, gains, tokens, weights):
    rows_here, feats = tokens[0].shape
    width = weights[0].shape[2]
    rows = weights[0].shape[1] // 4
    depth = 4 * feats
    return pl.pallas_call(
        functools.partial(project_kernel, rows),
        out_shape=(
            jax.ShapeDtypeStruct((rows_here, width), BF),
            jax.ShapeDtypeStruct((rows_here, 2 * width), BF),
        ),
        in_specs=[SMEM, SMEM, VMEM] + [ANY] * (5 + 16),
        out_specs=(VMEM, VMEM),
        scratch_shapes=[
            pltpu.VMEM((rows_here, depth), BF),
            pltpu.VMEM((3, depth, width), BF),
            pltpu.SemaphoreType.DMA((5,)),
            pltpu.SemaphoreType.DMA((16, 4)),
        ],
        compiler_params=pltpu.CompilerParams(vmem_limit_bytes=LIMIT),
        cost_estimate=pl.CostEstimate(
            flops=2 * rows_here * depth * 3 * width, bytes_accessed=12 * 2**20, transcendentals=0
        ),
        name="project",
    )(place, token_place, gains, *tokens, *weights)


def attend_frame(q, kv, keep, acc, heads, scale):
    rows, keys = q.shape[0], kv.shape[0]
    ones = jnp.ones((keys, HD), BF)
    out = []
    for h in range(heads):
        score = lax.dot_general(
            q[:, h * HD : (h + 1) * HD],
            kv[:, h * HD : (h + 1) * HD],
            (((1,), (1,)), ((), ())),
            preferred_element_type=jnp.float32,
        )
        weight = jnp.exp2(score * scale).reshape(rows // TILE, TILE, keys)
        weight = jnp.where(keep[:, None, :] > 0, weight, 0.0).reshape(rows, keys).astype(BF)
        at = (heads + h) * HD
        value = jnp.concatenate([kv[:, at : at + HD], ones], axis=1)
        part = jnp.dot(weight, value, preferred_element_type=jnp.float32)
        out.append(part if acc is None else acc[h] + part)
    return out


def own_kernel(heads, scale, q_ref, kv_ref, keep_ref, acc_ref):
    parts = attend_frame(q_ref, kv_ref, keep_ref[...], None, heads, scale)
    for h in range(heads):
        acc_ref[h] = parts[h]


def rest_kernel(heads, scale, q_ref, before_ref, after_ref, keep_ref, acc_ref, out_ref):
    keys = before_ref.shape[0]
    acc = [acc_ref[h] for h in range(heads)]
    acc = attend_frame(q_ref, before_ref, keep_ref[:, :keys], acc, heads, scale)
    acc = attend_frame(q_ref, after_ref, keep_ref[:, keys:], acc, heads, scale)
    for h in range(heads):
        out_ref[:, h * HD : (h + 1) * HD] = (acc[h][:, :HD] / acc[h][:, HD:]).astype(BF)


def local_call(kernel, out_shape, n_in, flops, nbytes, name):
    return pl.pallas_call(
        kernel,
        out_shape=out_shape,
        in_specs=[VMEM] * n_in,
        out_specs=VMEM,
        compiler_params=pltpu.CompilerParams(vmem_limit_bytes=LIMIT),
        cost_estimate=pl.CostEstimate(flops=flops, bytes_accessed=nbytes, transcendentals=0),
        name=name,
    )


def output_kernel(place, own, below, above, far_top, far_bottom, w_ref, out_ref, x, sem):
    feats = own.shape[1]
    half = far_top.shape[0]
    copies = []
    for i, (ref, start) in enumerate(
        ((own, 0), (below, 0), (above, 0), (far_top, 0), (far_bottom, half))
    ):
        at = pl.multiple_of(place[i], 128)
        copies.append(
            pltpu.make_async_copy(
                ref, x.at[pl.ds(start, ref.shape[0]), pl.ds(at, feats)], sem.at[i]
            )
        )
    for c in copies:
        c.start()
    for c in copies:
        c.wait()
    out_ref[...] = jnp.dot(x[...], w_ref[...], preferred_element_type=jnp.float32).astype(BF)


def output_projection(place, pieces, weight):
    rows, feats = pieces[0].shape
    depth, width = weight.shape
    return pl.pallas_call(
        output_kernel,
        out_shape=jax.ShapeDtypeStruct((rows, width), BF),
        in_specs=[SMEM] + [ANY] * 5 + [VMEM],
        out_specs=VMEM,
        scratch_shapes=[pltpu.VMEM((rows, depth), BF), pltpu.SemaphoreType.DMA((5,))],
        compiler_params=pltpu.CompilerParams(vmem_limit_bytes=LIMIT),
        cost_estimate=pl.CostEstimate(
            flops=2 * rows * depth * width, bytes_accessed=5 * 2**20, transcendentals=0
        ),
        name="output",
    )(place, *pieces, weight)


def per_device(tokens_in, qkv_weight, norm_gains, out_weight, neighbours):
    rows = tokens_in.shape[0]
    width = qkv_weight.shape[2]
    heads = width // HD
    tiles = rows // TILE
    core, seq, head = lax.axis_index("dp"), lax.axis_index("seq"), lax.axis_index("head")
    z, y = head // NY, head % NY
    half = qkv_weight.shape[0] // 2
    feats = tokens_in.shape[1]

    seq_of = jnp.stack([(seq + d) % 4 for d in (0, -1, 1, 2, 2)]).astype(jnp.int32)
    place = jnp.stack(
        row_table(z, y, core, half) + row_table(z, y, 1 - core, half)
    ).astype(jnp.int32)
    listed = neighbours[:, :, None] == (head * FRAME - FRAME + jnp.arange(3 * FRAME))[None, None, :]
    listed = listed & (neighbours >= 0)[:, :, None]
    keep = jnp.repeat(jnp.any(listed, axis=1), TILE, axis=1).astype(jnp.float32)
    keys = FRAME * TILE

    out_all = lax.all_gather(jnp.transpose(out_weight), "head", axis=0, tiled=True)
    mine = lax.dynamic_slice_in_dim(jnp.transpose(qkv_weight, (1, 0, 2)), core * half, half, axis=1)
    buffers = weight_buffers(mine)
    tokens = (tokens_in,) + ring_x(tokens_in)
    weights = buffers + [swapped(b) for b in buffers]
    query, kv = project(place, seq_of * feats, norm_gains, tokens, weights)

    n = lax.axis_size("head")
    before = lax.ppermute(kv, "head", [(i, i + 1) for i in range(n - 1)])
    after = lax.ppermute(kv, "head", [(i + 1, i) for i in range(n - 1)])
    scale = HD ** (-0.5) * math.log2(math.e)
    acc = local_call(
        functools.partial(own_kernel, heads, scale),
        jax.ShapeDtypeStruct((heads, rows, 2 * HD), jnp.float32),
        3, 6 * rows * keys * HD * heads, 3 * 2**20, "own_frame",
    )(query, kv, keep[:, keys : 2 * keys])
    sides = jnp.concatenate([keep[:, :keys], keep[:, 2 * keys :]], axis=1)
    head_out = local_call(
        functools.partial(rest_kernel, heads, scale),
        jax.ShapeDtypeStruct((rows, width), BF),
        5, 12 * rows * keys * HD * heads, 4 * 2**20, "other_frames",
    )(query, before, after, sides, acc)
    pieces = (head_out,) + ring_x(head_out)
    return output_projection(seq_of * width, pieces, out_all)


def solution(mesh):
    placed = (
        P(("dp", "head"), "seq"),
        P("head", None, "seq"),
        P(),
        P("seq", "head"),
        P(("dp", "head"), None),
    )
    return jax.shard_map(
        per_device, mesh=mesh, in_specs=placed, out_specs=P(("dp", "head"), "seq"), check_vma=False
    )
```

```python
import functools
import math

import jax
import jax.numpy as jnp
from jax import lax
from jax.experimental import pallas as pl
from jax.experimental.pallas import tpu as pltpu
from jax.sharding import PartitionSpec as P

HD = 128
TILE = 128
FRAME = 4
NY, NZ = 4, 8
BF = jnp.bfloat16
ANY = pl.BlockSpec(memory_space=pltpu.HBM)
VMEM = pl.BlockSpec(memory_space=pltpu.VMEM)
SMEM = pl.BlockSpec(memory_space=pltpu.SMEM)
LIMIT = 24 * 1024 * 1024
LARGE = 60 * 1024 * 1024

Y_FIRST_SUB = (0, -1, 1, 2)
Z_FIRST_SUB = (0, -2, 2, 4)
Y_FIRST_BUF = (0, -1, 1, -2, 2, -3, 3, -4)
Z_FIRST_BUF = ((0, 0), (1, 0), (0, 1), (1, -1), (0, 2), (1, -2), (0, 3), (1, -3))


def moved(x, core0, core1):
    pairs = []
    for core, (dz, dy) in enumerate((core0, core1)):
        for z in range(NZ):
            for y in range(NY):
                target = ((z + dz) % NZ) * NY + (y + dy) % NY
                pairs.append((core * NZ * NY + z * NY + y, core * NZ * NY + target))
    return lax.ppermute(x, ("dp", "head"), pairs)


def along(x, axis, step):
    n = lax.axis_size(axis)
    return lax.ppermute(x, axis, [(i, (i + step) % n) for i in range(n)])


def swapped(x):
    return lax.ppermute(x, "dp", [(0, 1), (1, 0)])


def ring_x(x):
    half = x.shape[0] // 2
    below = along(x, "seq", 1)
    above = along(x, "seq", -1)
    far_top = along(below[:half], "seq", 1)
    far_bottom = along(above[half:], "seq", -1)
    return below, above, far_top, far_bottom


def chain(start):
    p1 = moved(start, (1, 0), (-1, 0))
    p2 = moved(start, (-1, 0), (0, -1))
    p3 = moved(p1, (1, 0), (0, 1))
    p4 = moved(p2, (-1, 0), (0, -1))
    p5 = moved(p3, (1, 0), (0, 1))
    p6 = moved(p4, (-1, 0), (0, -1))
    p7 = moved(p5, (1, 0), (0, 1))
    return [start, p1, p2, p3, p4, p5, p6, p7]


def gathered(tokens, mine):
    half = tokens.shape[0] // 2
    top, bottom = tokens[:half], tokens[half:]
    below_top = along(top, "seq", 1)
    above_bottom = along(bottom, "seq", -1)
    a = moved(mine, (0, 1), (2, 0))
    b = moved(mine, (0, -1), (-2, 0))
    c = moved(mine, (0, 2), (4, 0))
    below_top, above_bottom, a, b, c = lax.optimization_barrier(
        (below_top, above_bottom, a, b, c)
    )
    far_top = along(below_top, "seq", 1)
    far_bottom = along(above_bottom, "seq", -1)
    below_bottom = along(bottom, "seq", 1)
    above_top = along(top, "seq", -1)
    sets = []
    for j in (0, 2):
        start = jnp.concatenate([x[j : j + 2] for x in (mine, a, b, c)], axis=1)
        buffers = chain(start)
        sets.append(buffers + [swapped(x) for x in buffers])
    pieces = (tokens, below_top, below_bottom, above_top, above_bottom, far_top, far_bottom)
    return pieces, sets


def row_table(z, y, core, rows):
    table = []
    for k in range(8):
        for i in range(4):
            z0, y0 = (z + Y_FIRST_BUF[k]) % NZ, (y + Y_FIRST_SUB[i]) % NY
            z1 = (z + Z_FIRST_BUF[k][0] + Z_FIRST_SUB[i]) % NZ
            y1 = (y + Z_FIRST_BUF[k][1]) % NY
            block = jnp.where(core == 0, z0 * NY + y0, z1 * NY + y1)
            table.append((block * 2 + core) * rows)
    return table


def normed(values, gain):
    mean_sq = jnp.mean(values * values, axis=-1, keepdims=True)
    return (values * lax.rsqrt(mean_sq + 1e-06) * gain).astype(BF)


def weight_copies(rows, place, refs, target, sem, item):
    copies = []
    for k, ref in enumerate(refs):
        for i in range(4):
            at = pl.multiple_of(place[k * 4 + i], 16)
            copies.append(
                pltpu.make_async_copy(
                    ref.at[item, pl.ds(i * rows, rows), :], target(at, k), sem.at[k, i]
                )
            )
    return copies


def kv_kernel(rows, place, token_place, *refs):
    gains = refs[0]
    tokens = refs[1:8]
    weights = refs[8:24]
    kv_ref, x = refs[24:26]
    w, x_sem, k_sem, v_sem = refs[26:]
    feats = tokens[0].shape[1]
    half = tokens[1].shape[0]
    token_copies = []
    starts = (0, 0, half, 0, half, 0, half)
    for i, ref in enumerate(tokens):
        n = ref.shape[0]
        at = pl.multiple_of(token_place[i], 128)
        token_copies.append(
            pltpu.make_async_copy(ref, x.at[pl.ds(starts[i], n), pl.ds(at, feats)], x_sem.at[i])
        )
    k_copies = weight_copies(rows, place, weights, lambda at, k: w.at[0, pl.ds(at, rows), :], k_sem, 0)
    v_copies = weight_copies(rows, place, weights, lambda at, k: w.at[1, pl.ds(at, rows), :], v_sem, 1)
    for c in token_copies + k_copies + v_copies:
        c.start()
    for c in token_copies + k_copies:
        c.wait()
    width = w.shape[2]
    heads = width // HD
    out = jnp.dot(x[...], w[0], preferred_element_type=jnp.float32)
    for h in range(heads):
        at = h * HD
        kv_ref[:, at : at + HD] = normed(out[:, at : at + HD], gains[1:2, :])
    for c in v_copies:
        c.wait()
    out = jnp.dot(x[...], w[1], preferred_element_type=jnp.float32)
    kv_ref[:, width:] = out.astype(BF)


def project_kv(place, token_place, gains, tokens, weights):
    rows_here, feats = tokens[0].shape
    width = weights[0].shape[2]
    rows = weights[0].shape[1] // 4
    depth = 4 * feats
    return pl.pallas_call(
        functools.partial(kv_kernel, rows),
        out_shape=(
            jax.ShapeDtypeStruct((rows_here, 2 * width), BF),
            jax.ShapeDtypeStruct((rows_here, depth), BF),
        ),
        in_specs=[SMEM, SMEM, VMEM] + [ANY] * (7 + 16),
        out_specs=(VMEM, VMEM),
        scratch_shapes=[
            pltpu.VMEM((2, depth, width), BF),
            pltpu.SemaphoreType.DMA((7,)),
            pltpu.SemaphoreType.DMA((16, 4)),
            pltpu.SemaphoreType.DMA((16, 4)),
        ],
        compiler_params=pltpu.CompilerParams(vmem_limit_bytes=LARGE),
        cost_estimate=pl.CostEstimate(
            flops=4 * rows_here * depth * width, bytes_accessed=8 * 2**20, transcendentals=0
        ),
        name="project_kv",
    )(place, token_place, gains, *tokens, *weights)


def attend_frame(q, kv, keep, acc, heads, scale):
    rows, keys = q.shape[0], kv.shape[0]
    ones = jnp.ones((keys, HD), BF)
    out = []
    for h in range(heads):
        score = lax.dot_general(
            q[:, h * HD : (h + 1) * HD],
            kv[:, h * HD : (h + 1) * HD],
            (((1,), (1,)), ((), ())),
            preferred_element_type=jnp.float32,
        )
        weight = jnp.exp2(score * scale).reshape(rows // TILE, TILE, keys)
        weight = jnp.where(keep[:, None, :] > 0, weight, 0.0).reshape(rows, keys).astype(BF)
        at = (heads + h) * HD
        value = jnp.concatenate([kv[:, at : at + HD], ones], axis=1)
        part = jnp.dot(weight, value, preferred_element_type=jnp.float32)
        out.append(part if acc is None else acc[h] + part)
    return out


def own_kernel(rows, scale, place, x, kv_ref, keep_ref, gains, *refs):
    weights = refs[:16]
    q_ref, acc_ref, out_w = refs[16:19]
    w, q_sem, o_sem = refs[19:]
    out_rows, out_cols = out_w.shape
    depth, width = w.shape
    q_copies = weight_copies(rows, place, weights, lambda at, k: w.at[pl.ds(at, rows), :], q_sem, 0)
    core = place[64]

    o_copies = []
    for k, ref in enumerate(weights):
        side = core if k < 8 else 1 - core
        for i in range(4):
            row = pl.multiple_of(place[65 + 4 * k + i], 16)
            col = pl.multiple_of(side * width, 128)
            o_copies.append(
                pltpu.make_async_copy(
                    ref.at[1, pl.ds(i * rows, rows), :],
                    out_w.at[pl.ds(row, rows), pl.ds(col, width)],
                    o_sem.at[k, i],
                )
            )
    for c in q_copies + o_copies:
        c.start()
    for c in q_copies:
        c.wait()
    heads = width // HD
    out = jnp.dot(x[...], w[...], preferred_element_type=jnp.float32)
    for h in range(heads):
        at = h * HD
        q_ref[:, at : at + HD] = normed(out[:, at : at + HD], gains[0:1, :])
    parts = attend_frame(q_ref, kv_ref, keep_ref[...], None, heads, scale)
    for h in range(heads):
        acc_ref[h] = parts[h]
    for c in o_copies:
        c.wait()


def own_frame(place, x, kv, keep, gains, weights, out_shape, scale):
    rows_here, depth = x.shape
    width = weights[0].shape[2]
    rows = weights[0].shape[1] // 4
    heads = width // HD
    return pl.pallas_call(
        functools.partial(own_kernel, rows, scale),
        out_shape=(
            jax.ShapeDtypeStruct((rows_here, width), BF),
            jax.ShapeDtypeStruct((heads, rows_here, 2 * HD), jnp.float32),
            jax.ShapeDtypeStruct(out_shape, BF),
        ),
        in_specs=[SMEM] + [VMEM] * 4 + [ANY] * 16,
        out_specs=(VMEM,) * 3,
        scratch_shapes=[
            pltpu.VMEM((depth, width), BF),
            pltpu.SemaphoreType.DMA((16, 4)),
            pltpu.SemaphoreType.DMA((16, 4)),
        ],
        compiler_params=pltpu.CompilerParams(vmem_limit_bytes=LARGE),
        cost_estimate=pl.CostEstimate(
            flops=2 * rows_here * depth * width, bytes_accessed=8 * 2**20, transcendentals=0
        ),
        name="own_frame",
    )(place, x, kv, keep, gains, *weights)


def rest_kernel(heads, scale, q_ref, before_ref, after_ref, keep_ref, acc_ref, out_ref):
    keys = before_ref.shape[0]
    acc = [acc_ref[h] for h in range(heads)]
    acc = attend_frame(q_ref, before_ref, keep_ref[:, :keys], acc, heads, scale)
    acc = attend_frame(q_ref, after_ref, keep_ref[:, keys:], acc, heads, scale)
    for h in range(heads):
        out_ref[:, h * HD : (h + 1) * HD] = (acc[h][:, :HD] / acc[h][:, HD:]).astype(BF)


def local_call(kernel, out_shape, n_in, flops, nbytes, name):
    return pl.pallas_call(
        kernel,
        out_shape=out_shape,
        in_specs=[VMEM] * n_in,
        out_specs=VMEM,
        compiler_params=pltpu.CompilerParams(vmem_limit_bytes=LIMIT),
        cost_estimate=pl.CostEstimate(flops=flops, bytes_accessed=nbytes, transcendentals=0),
        name=name,
    )


def output_kernel(place, own, below, above, far_top, far_bottom, w_ref, out_ref, x, sem):
    feats = own.shape[1]
    half = far_top.shape[0]
    copies = []
    for i, (ref, start) in enumerate(
        ((own, 0), (below, 0), (above, 0), (far_top, 0), (far_bottom, half))
    ):
        at = pl.multiple_of(place[i], 128)
        copies.append(
            pltpu.make_async_copy(
                ref, x.at[pl.ds(start, ref.shape[0]), pl.ds(at, feats)], sem.at[i]
            )
        )
    for c in copies:
        c.start()
    for c in copies:
        c.wait()
    out_ref[...] = jnp.dot(x[...], w_ref[...], preferred_element_type=jnp.float32).astype(BF)


def output_projection(place, pieces, weight):
    rows, feats = pieces[0].shape
    depth, width = weight.shape
    return pl.pallas_call(
        output_kernel,
        out_shape=jax.ShapeDtypeStruct((rows, width), BF),
        in_specs=[SMEM] + [ANY] * 5 + [VMEM],
        out_specs=VMEM,
        scratch_shapes=[pltpu.VMEM((rows, depth), BF), pltpu.SemaphoreType.DMA((5,))],
        compiler_params=pltpu.CompilerParams(vmem_limit_bytes=LIMIT),
        cost_estimate=pl.CostEstimate(
            flops=2 * rows * depth * width, bytes_accessed=5 * 2**20, transcendentals=0
        ),
        name="output",
    )(place, *pieces, weight)


def per_device(tokens_in, qkv_weight, norm_gains, out_weight, neighbours):
    rows = tokens_in.shape[0]
    width = qkv_weight.shape[2]
    heads = width // HD
    tiles = rows // TILE
    core, seq, head = lax.axis_index("dp"), lax.axis_index("seq"), lax.axis_index("head")
    z, y = head // NY, head % NY
    half = qkv_weight.shape[0] // 2
    feats = tokens_in.shape[1]

    seq_of = jnp.stack([(seq + d) % 4 for d in (0, -1, -1, 1, 1, 2, 2)]).astype(jnp.int32)
    rows_of = jnp.stack(row_table(z, y, core, half) + row_table(z, y, 1 - core, half))
    rows_of = rows_of.astype(jnp.int32)
    places = jnp.concatenate([rows_of, core[None].astype(jnp.int32), rows_of // (2 * half) * half])
    listed = neighbours[:, :, None] == (head * FRAME - FRAME + jnp.arange(3 * FRAME))[None, None, :]
    listed = listed & (neighbours >= 0)[:, :, None]
    keep = jnp.repeat(jnp.any(listed, axis=1), TILE, axis=1).astype(jnp.float32)
    keys = FRAME * TILE

    mine = lax.dynamic_slice_in_dim(jnp.transpose(qkv_weight, (1, 0, 2)), core * half, half, axis=1)
    mine_out = lax.dynamic_slice_in_dim(jnp.transpose(out_weight), core * width, width, axis=1)
    mine = jnp.concatenate([mine[1:], mine[:1], mine_out[None]], axis=0)
    tokens, (kv_weights, q_weights) = gathered(tokens_in, mine)
    kv, x = project_kv(rows_of, seq_of * feats, norm_gains, tokens, kv_weights)

    n = lax.axis_size("head")
    before = lax.ppermute(kv, "head", [(i, i + 1) for i in range(n - 1)])
    after = lax.ppermute(kv, "head", [(i + 1, i) for i in range(n - 1)])
    scale = HD ** (-0.5) * math.log2(math.e)
    query, acc, out_all = own_frame(
        places, x, kv, keep[:, keys : 2 * keys], norm_gains, q_weights, (4 * width, feats), scale
    )
    sides = jnp.concatenate([keep[:, :keys], keep[:, 2 * keys :]], axis=1)
    head_out = local_call(
        functools.partial(rest_kernel, heads, scale),
        jax.ShapeDtypeStruct((rows, width), BF),
        5, 12 * rows * keys * HD * heads, 4 * 2**20, "other_frames",
    )(query, before, after, sides, acc)
    pieces = (head_out,) + ring_x(head_out)
    return output_projection(seq_of[jnp.array([0, 1, 3, 5, 6])] * width, pieces, out_all)


def solution(mesh):
    placed = (
        P(("dp", "head"), "seq"),
        P("head", None, "seq"),
        P(),
        P("seq", "head"),
        P(("dp", "head"), None),
    )
    return jax.shard_map(
        per_device, mesh=mesh, in_specs=placed, out_specs=P(("dp", "head"), "seq"), check_vma=False
    )
```

```python
import functools
import math

import jax
import jax.numpy as jnp
from jax import lax
from jax.experimental import pallas as pl
from jax.experimental.pallas import tpu as pltpu
from jax.sharding import PartitionSpec as P

HD = 128
TILE = 128
FRAME = 4
NX, NY, NZ = 4, 4, 8
BF = jnp.bfloat16
F32 = jnp.float32
VMEM = pl.BlockSpec(memory_space=pltpu.VMEM)

SUB_0 = ((0, 0), (0, -1), (0, 1), (0, 2))
SUB_1 = ((0, 0), (-2, 0), (2, 0), (4, 0))
BUF_0 = ((0, 0), (-1, 0), (1, 0), (-2, 0), (2, 0), (-3, 0), (3, 0), (-4, 0))
BUF_1 = ((0, 0), (1, 0), (0, 1), (1, -1), (0, 2), (1, -2), (0, 3), (1, -3))
GROUPS = ((0, 1), (2,))


def moved(x, core0, core1):
    pairs = []
    for core, (dz, dy) in enumerate((core0, core1)):
        for z in range(NZ):
            for y in range(NY):
                target = ((z + dz) % NZ) * NY + (y + dy) % NY
                pairs.append((core * NZ * NY + z * NY + y, core * NZ * NY + target))
    return lax.ppermute(x, ("dp", "head"), pairs)


def frames_on(x, step):
    n = NZ * NY
    return lax.ppermute(x, "head", [(i, (i + step) % n) for i in range(n)])


def along(x, axis, step):
    n = lax.axis_size(axis)
    return lax.ppermute(x, axis, [(i, (i + step) % n) for i in range(n)])


def swapped(x):
    return lax.ppermute(x, "dp", [(0, 1), (1, 0)])


def halves_kernel(below, above, top, bottom):
    half = top.shape[0]
    top[...] = below[:half, :]
    bottom[...] = above[half:, :]


def halves(below, above):
    shape = jax.ShapeDtypeStruct((below.shape[0] // 2, below.shape[1]), BF)
    return call(halves_kernel, (shape, shape), (below, above), [], 2**34, 2**20, 8, "halves")


def gathered(tokens, both):
    below = along(tokens, "seq", 1)
    above = along(tokens, "seq", -1)
    a = moved(both, (0, 1), (2, 0))
    b = moved(both, (0, -1), (-2, 0))
    c = moved(both, (0, 2), (4, 0))
    s = jnp.concatenate([both, a, b, c], axis=1)
    p1 = moved(s, (1, 0), (-1, 0))
    top, bottom = halves(below, above)
    below, above, top, bottom, p1, s = lax.optimization_barrier(
        (below, above, top, bottom, p1, s)
    )
    far_top = along(top, "seq", 1)
    far_bottom = along(bottom, "seq", -1)
    p3, p2 = moved(p1, (1, 0), (0, 1)), moved(s, (-1, 0), (0, -1))
    p5, p4 = moved(p3, (1, 0), (0, 1)), moved(p2, (-1, 0), (0, -1))
    far_top, far_bottom, p5, p4 = lax.optimization_barrier((far_top, far_bottom, p5, p4))
    p7, p6 = moved(p5, (1, 0), (0, 1)), moved(p4, (-1, 0), (0, -1))
    return (tokens, below, above, far_top, far_bottom), (s, p1, p2, p3, p4, p5, p6, p7)


def prepare_kernel(columns, out_w, both):
    core = lax.axis_index("dp")
    rows, cols = out_w.shape[0], columns.shape[2]
    both[0] = jnp.where(core == 0, columns[1], columns[2])

    @pl.when(core == 0)
    def _():
        both[1] = columns[0]

    @pl.when(core == 1)
    def _():
        both[1, :rows, :] = out_w[:, :cols]
        both[1, rows:, :] = out_w[:, cols:]


def place():
    head = lax.axis_index("head")
    return lax.axis_index("dp"), lax.axis_index("seq"), lax.div(head, NY), lax.rem(head, NY)


def block_of(z, y, core, k, i):
    z0, y0 = BUF_0[k][0] + SUB_0[i][0], BUF_0[k][1] + SUB_0[i][1]
    z1, y1 = BUF_1[k][0] + SUB_1[i][0], BUF_1[k][1] + SUB_1[i][1]
    dz = jnp.where(core == 0, z0 % NZ, z1 % NZ)
    dy = jnp.where(core == 0, y0 % NY, y1 % NY)
    return lax.rem(z + dz, NZ) * NY + lax.rem(y + dy, NY)


def normed(values, gain):
    mean_sq = jnp.mean(values * values, axis=-1, keepdims=True)
    return (values * lax.rsqrt(mean_sq + 1e-06) * gain).astype(BF)


def call(kernel, out_shape, args, scratch, flops, nbytes, limit, name):
    n = len(args)
    many = isinstance(out_shape, tuple)
    return pl.pallas_call(
        kernel,
        out_shape=out_shape,
        in_specs=[VMEM] * n,
        out_specs=(VMEM,) * len(out_shape) if many else VMEM,
        scratch_shapes=scratch,
        compiler_params=pltpu.CompilerParams(vmem_limit_bytes=limit * 2**20),
        cost_estimate=pl.CostEstimate(flops=flops, bytes_accessed=nbytes, transcendentals=0),
        name=name,
    )(*args)


def assemble(w, buffers, item, core, z, y):
    rows = buffers[0].shape[1] // 4
    for k, ref in enumerate(buffers):
        for i in range(4):
            at = pl.multiple_of(block_of(z, y, core, k, i) * rows, 16)
            w[pl.ds(at, rows), :] = ref[item, i * rows : (i + 1) * rows, :]


def multiply_tokens(pieces, w, seq, store):
    own, below, above, far_top, far_bottom = pieces
    feats, half = own.shape[1], far_top.shape[0]

    def part(ref, step):
        at = pl.multiple_of(lax.rem(seq + step, NX) * feats, 128)
        return jnp.dot(ref[...], w[pl.ds(at, feats), :], preferred_element_type=F32)

    near = part(own, 0) + part(below, 3) + part(above, 1)
    store(slice(0, half), near[:half] + part(far_top, 2))
    store(slice(half, 2 * half), near[half:] + part(far_bottom, 2))


def kv_store(out, core, gains):
    def store(rows, product):
        for h in range(product.shape[1] // HD):
            at = slice(h * HD, (h + 1) * HD)
            part = product[:, at]
            out[rows, at] = jnp.where(core == 0, normed(part, gains[1:2, :]), part.astype(BF))

    return store


def cross_kernel(gains, *refs):
    pieces, buffers = refs[:5], refs[5:13]
    out, w = refs[13:]
    core, seq, z, y = place()
    assemble(w, buffers, 0, core, z, y)
    multiply_tokens(pieces, w, seq, kv_store(out, core, gains))


def same_kernel(gains, *refs):
    pieces, w, out = refs[:5], refs[5], refs[6]
    core, seq, _, _ = place()
    multiply_tokens(pieces, w, seq, kv_store(out, core, gains))


def pack_kernel(a, b, *outs):
    core = lax.axis_index("dp")
    for out, group in zip(outs, GROUPS, strict=True):
        at = slice(group[0] * HD, (group[-1] + 1) * HD)
        size = len(group) * HD
        out[:, :size] = jnp.where(core == 0, a[:, at], b[:, at])
        out[:, size:] = jnp.where(core == 0, b[:, at], a[:, at])


def project_kv(gains, tokens, others, buffers):
    rows, feats = tokens[0].shape
    depth, width = NX * feats, buffers[0].shape[2]
    part = jax.ShapeDtypeStruct((rows, width), BF)
    flops = 2 * rows * depth * width
    cross, w = call(
        cross_kernel, (part, jax.ShapeDtypeStruct((depth, width), BF)),
        (gains, *others, *buffers), [], flops, 6 * 2**20, 20, "project_cross",
    )
    cross = swapped(cross)
    same = call(same_kernel, part, (gains, *tokens, w), [], 8 * flops, 6 * 2**20, 20, "project_same")
    return call(
        pack_kernel,
        tuple(jax.ShapeDtypeStruct((rows, 2 * len(g) * HD), BF) for g in GROUPS),
        (same, cross), [], 0, 2**21, 8, "pack",
    )


def q_kernel(gains, *refs):
    sides = (refs[:5], refs[5:10])
    buffers = refs[10:18]
    q_refs = refs[18:20]
    out_w, w = refs[20:]
    core, seq, z, y = place()

    @pl.when(core == 0)
    def _():
        assemble(w, buffers, 1, core, z, y)
        for side, pieces in enumerate(sides):

            def store(rows, product, side=side):
                for h in range(product.shape[1] // HD):
                    at = slice(h * HD, (h + 1) * HD)
                    q_refs[side][rows, at] = normed(product[:, at], gains[0:1, :])

            multiply_tokens(pieces, w, seq, store)

    @pl.when(core == 1)
    def _():
        rows, cols = buffers[0].shape[1] // 8, buffers[0].shape[2]
        for k, ref in enumerate(buffers):
            for i in range(4):
                at = pl.multiple_of(block_of(z, y, core, k, i) * rows, 16)
                for j in range(2):
                    first = (2 * i + j) * rows
                    out_w[pl.ds(at, rows), j * cols : (j + 1) * cols] = ref[1, first : first + rows, :]


def project_q(gains, tokens, others, buffers):
    rows, feats = tokens[0].shape
    depth, width = NX * feats, buffers[0].shape[2]
    query = jax.ShapeDtypeStruct((rows, width), BF)
    return call(
        q_kernel,
        (query, query, jax.ShapeDtypeStruct((NX * width, feats), BF)),
        (gains, *tokens, *others, *buffers),
        [pltpu.VMEM((depth, width), BF)],
        32 * rows * depth * width, 9 * 2**20, 20, "project_q",
    )


def attend_frame(scale, q, kv, keep, n):
    rows, keys = q.shape[0], kv.shape[0]
    at, size = n * HD, kv.shape[1] // 2
    score = lax.dot_general(
        q, kv[:, at : at + HD], (((1,), (1,)), ((), ())), preferred_element_type=F32
    )
    weight = jnp.exp2(score * scale).reshape(rows // TILE, TILE, keys)
    weight = jnp.where(keep[:, None, :] > 0, weight, 0.0).reshape(rows, keys).astype(BF)
    value = jnp.concatenate([kv[:, size + at : size + at + HD], jnp.ones((keys, HD), BF)], axis=1)
    return jnp.dot(weight, value, preferred_element_type=F32)


def kept(listed, frame, keys):
    tiles = listed.shape[0]
    lane = lax.div(lax.broadcasted_iota(jnp.int32, (tiles, keys), 1), TILE)
    tile = lane + frame * FRAME
    keep = jnp.zeros((tiles, keys), jnp.bool_)
    for s in range(listed.shape[1]):
        keep = keep | (tile == listed[:, s : s + 1])
    return jnp.where(keep & (tile >= 0), 1.0, 0.0)


def attend_kernel(scale, group, near, q_own, q_other, own, before, after, out):
    core, head = lax.axis_index("dp"), lax.axis_index("head")
    keep = [kept(near[...], head + step, q_own.shape[0]) for step in (0, -1, 1)]
    for n, h in enumerate(group):
        at = slice(h * HD, (h + 1) * HD)
        q = jnp.where(core == 0, q_own[:, at], q_other[:, at])
        total = attend_frame(scale, q, own, keep[0], n)
        total = total + attend_frame(scale, q, before, keep[1], n)
        total = total + attend_frame(scale, q, after, keep[2], n)
        out[:, n * HD : (n + 1) * HD] = (total[:, :HD] / total[:, HD:]).astype(BF)


def output_kernel(group, w_own, w_other, total, *refs):
    pieces, out = refs[:-1], refs[-1]
    core, seq = lax.axis_index("dp"), lax.axis_index("seq")
    width = w_own.shape[0] // NX
    size = len(group) * HD

    def part(ref, step):
        at = pl.multiple_of(lax.rem(seq + step, NX) * width + group[0] * HD, HD)
        w = jnp.where(core == 1, w_own[pl.ds(at, size), :], w_other[pl.ds(at, size), :])
        return jnp.dot(ref[...], w, preferred_element_type=F32)

    near = part(pieces[0], 0) + part(pieces[1], 3) + part(pieces[2], 1)
    if total is not None:
        near = near + total[...]
    start = 0
    for far in pieces[3:]:
        rows = slice(start, start + far.shape[0])
        out[rows, :] = (near[rows] + part(far, 2)).astype(out.dtype)
        start += far.shape[0]


def first_kernel(group, w_own, w_other, *refs):
    output_kernel(group, w_own, w_other, None, *refs)


def ring_x(x):
    half = x.shape[0] // 2
    below = along(x, "seq", 1)
    above = along(x, "seq", -1)
    return x, below, above, along(below[:half], "seq", 1), along(above[half:], "seq", -1)


def direct_x(x):
    return x, along(x, "seq", 1), along(x, "seq", -1), along(x, "seq", 2)


def per_device(tokens_in, qkv_weight, norm_gains, out_weight, neighbours):
    rows, feats = tokens_in.shape
    width = qkv_weight.shape[2]
    heads = width // HD
    both = call(
        prepare_kernel, jax.ShapeDtypeStruct((2, qkv_weight.shape[0], width), BF),
        (jnp.transpose(qkv_weight, (1, 0, 2)), jnp.transpose(out_weight)),
        [], 2**35, 2**20, 8, "prepare",
    )
    tokens, buffers = gathered(tokens_in, both)
    others = tuple(swapped(x) for x in tokens)

    kv = project_kv(norm_gains, tokens, others, buffers)
    sides = [[frames_on(x, step) for step in (1, -1)] for x in kv]
    gains, *kv = lax.optimization_barrier((norm_gains, *kv))
    q_own, q_cross, out_w = project_q(gains, tokens, others, buffers)
    q_other, w_other = swapped(q_cross), swapped(out_w)

    scale = HD ** (-0.5) * math.log2(math.e)
    total = ()
    for g, group in enumerate(GROUPS):
        last = g == len(GROUPS) - 1
        out = call(
            functools.partial(attend_kernel, scale, group),
            jax.ShapeDtypeStruct((rows, len(group) * HD), BF),
            (neighbours, q_own, q_other, kv[g], *sides[g]),
            [], 18 * rows * rows * HD * len(group), 4 * 2**20, 16, "attend_%d" % g,
        )
        pieces = (direct_x if last and g else ring_x)(out)
        total = (
            call(
                functools.partial(output_kernel if g else first_kernel, group),
                jax.ShapeDtypeStruct((rows, feats), BF if last else F32),
                (out_w, w_other, *total, *pieces),
                [], 8 * rows * feats * len(group) * HD, 5 * 2**20, 16, "output_%d" % g,
            ),
        )
    return total[0]


def solution(mesh):
    placed = (
        P(("dp", "head"), "seq"),
        P("head", None, "seq"),
        P(),
        P("seq", "head"),
        P(("dp", "head"), None),
    )
    return jax.shard_map(
        per_device, mesh=mesh, in_specs=placed, out_specs=P(("dp", "head"), "seq"), check_vma=False
    )
```

```python
import functools
import math

import jax
import jax.numpy as jnp
from jax import lax
from jax.experimental import pallas as pl
from jax.experimental.pallas import tpu as pltpu
from jax.sharding import PartitionSpec as P

HD = 128
TILE = 128
FRAME = 4
NX, NY, NZ = 4, 4, 8
BF = jnp.bfloat16
F32 = jnp.float32
VMEM = pl.BlockSpec(memory_space=pltpu.VMEM)

SUB_0 = ((0, 0), (0, -1), (0, 1), (0, 2))
SUB_1 = ((0, 0), (-2, 0), (2, 0), (4, 0))
BUF_0 = ((0, 0), (-1, 0), (1, 0), (-2, 0), (2, 0), (-3, 0), (3, 0), (-4, 0))
BUF_1 = ((0, 0), (1, 0), (0, 1), (1, -1), (0, 2), (1, -2), (0, 3), (1, -3))
GROUPS = ((0, 1), (2,))


def moved(x, core0, core1):
    pairs = []
    for core, (dz, dy) in enumerate((core0, core1)):
        for z in range(NZ):
            for y in range(NY):
                target = ((z + dz) % NZ) * NY + (y + dy) % NY
                pairs.append((core * NZ * NY + z * NY + y, core * NZ * NY + target))
    return lax.ppermute(x, ("dp", "head"), pairs)


def frames_on(x, step):
    n = NZ * NY
    return lax.ppermute(x, "head", [(i, (i + step) % n) for i in range(n)])


def along(x, axis, step):
    n = lax.axis_size(axis)
    return lax.ppermute(x, axis, [(i, (i + step) % n) for i in range(n)])


def swapped(x):
    return lax.ppermute(x, "dp", [(0, 1), (1, 0)])


def halves_kernel(below, above, top, bottom):
    half = top.shape[0]
    top[...] = below[:half, :]
    bottom[...] = above[half:, :]


def halves(below, above):
    shape = jax.ShapeDtypeStruct((below.shape[0] // 2, below.shape[1]), BF)
    return call(halves_kernel, (shape, shape), (below, above), [], 2**34, 2**20, 8, "halves")


def gathered(tokens, mine):
    below = along(tokens, "seq", 1)
    above = along(tokens, "seq", -1)
    a = moved(mine, (0, 1), (2, 0))
    b = moved(mine, (0, -1), (-2, 0))
    c = moved(mine, (0, 2), (4, 0))
    s = jnp.concatenate([mine, a, b, c], axis=0)
    p1 = moved(s, (1, 0), (-1, 0))
    top, bottom = halves(below, above)
    below, above, top, bottom, p1, s = lax.optimization_barrier(
        (below, above, top, bottom, p1, s)
    )
    far_top = along(top, "seq", 1)
    far_bottom = along(bottom, "seq", -1)
    p3, p2 = moved(p1, (1, 0), (0, 1)), moved(s, (-1, 0), (0, -1))
    p5, p4 = moved(p3, (1, 0), (0, 1)), moved(p2, (-1, 0), (0, -1))
    pieces = (tokens, below, above, far_top, far_bottom)
    others = tuple(swapped(x) for x in pieces)
    *others, p5, p4 = lax.optimization_barrier((*others, p5, p4))
    p7, p6 = moved(p5, (1, 0), (0, 1)), moved(p4, (-1, 0), (0, -1))
    return pieces, others, (s, p1, p2, p3, p4, p5, p6, p7)


def prepare_kernel(columns, out_w, mine):
    core = lax.axis_index("dp")
    rows, cols = columns.shape[1:]
    half = rows // 2
    mine[:rows, :] = jnp.where(core == 0, columns[1], columns[2])
    mine[rows : rows + half, :] = jnp.where(core == 0, columns[0, :half, :], columns[0, half:, :])
    mine[rows + half :, :] = jnp.where(core == 0, out_w[:, :cols], out_w[:, cols:])


def place():
    head = lax.axis_index("head")
    return lax.axis_index("dp"), lax.axis_index("seq"), lax.div(head, NY), lax.rem(head, NY)


def block_of(z, y, core, k, i):
    z0, y0 = BUF_0[k][0] + SUB_0[i][0], BUF_0[k][1] + SUB_0[i][1]
    z1, y1 = BUF_1[k][0] + SUB_1[i][0], BUF_1[k][1] + SUB_1[i][1]
    dz = jnp.where(core == 0, z0 % NZ, z1 % NZ)
    dy = jnp.where(core == 0, y0 % NY, y1 % NY)
    return lax.rem(z + dz, NZ) * NY + lax.rem(y + dy, NY)


def normed(values, gain):
    mean_sq = jnp.mean(values * values, axis=-1, keepdims=True)
    return (values * lax.rsqrt(mean_sq + 1e-06) * gain).astype(BF)


def call(kernel, out_shape, args, scratch, flops, nbytes, limit, name):
    n = len(args)
    many = isinstance(out_shape, tuple)
    return pl.pallas_call(
        kernel,
        out_shape=out_shape,
        in_specs=[VMEM] * n,
        out_specs=(VMEM,) * len(out_shape) if many else VMEM,
        scratch_shapes=scratch,
        compiler_params=pltpu.CompilerParams(vmem_limit_bytes=limit * 2**20),
        cost_estimate=pl.CostEstimate(flops=flops, bytes_accessed=nbytes, transcendentals=0),
        name=name,
    )(*args)


def assemble(w, buffers, first, rows, core, z, y):
    size = buffers[0].shape[0] // 4
    for k, ref in enumerate(buffers):
        for i in range(4):
            at = pl.multiple_of(block_of(z, y, core, k, i) * rows, 16)
            start = i * size + first
            w[pl.ds(at, rows), :] = ref[start : start + rows, :]


def multiply_tokens(pieces, w, seq, store):
    own, below, above, far_top, far_bottom = pieces
    feats, half = own.shape[1], far_top.shape[0]

    def part(ref, step):
        at = pl.multiple_of(lax.rem(seq + step, NX) * feats, 128)
        return jnp.dot(ref[...], w[pl.ds(at, feats), :], preferred_element_type=F32)

    near = part(own, 0) + part(below, 3) + part(above, 1)
    store(slice(0, half), near[:half] + part(far_top, 2))
    store(slice(half, 2 * half), near[half:] + part(far_bottom, 2))


def kv_store(out, core, gains):
    def store(rows, product):
        for h in range(product.shape[1] // HD):
            at = slice(h * HD, (h + 1) * HD)
            part = product[:, at]
            out[rows, at] = jnp.where(core == 0, normed(part, gains[1:2, :]), part.astype(BF))

    return store


def cross_kernel(gains, *refs):
    pieces, buffers = refs[:5], refs[5:13]
    out, w = refs[13:]
    core, seq, z, y = place()
    rows = w.shape[0] // (NZ * NY)
    assemble(w, buffers, 0, rows, core, z, y)
    multiply_tokens(pieces, w, seq, kv_store(out, core, gains))


def same_kernel(gains, *refs):
    pieces, w, out = refs[:5], refs[5], refs[6]
    core, seq, _, _ = place()
    multiply_tokens(pieces, w, seq, kv_store(out, core, gains))


def pack_kernel(a, b, *outs):
    core = lax.axis_index("dp")
    for out, group in zip(outs, GROUPS, strict=True):
        at = slice(group[0] * HD, (group[-1] + 1) * HD)
        size = len(group) * HD
        out[:, :size] = jnp.where(core == 0, a[:, at], b[:, at])
        out[:, size:] = jnp.where(core == 0, b[:, at], a[:, at])


def project_kv(gains, tokens, others, buffers):
    rows, feats = tokens[0].shape
    depth, width = NX * feats, buffers[0].shape[1]
    part = jax.ShapeDtypeStruct((rows, width), BF)
    flops = 2 * rows * depth * width
    cross, w = call(
        cross_kernel, (part, jax.ShapeDtypeStruct((depth, width), BF)),
        (gains, *others, *buffers), [], flops, 6 * 2**20, 20, "project_cross",
    )
    cross = swapped(cross)
    same = call(same_kernel, part, (gains, *tokens, w), [], 8 * flops, 6 * 2**20, 20, "project_same")
    return call(
        pack_kernel,
        tuple(jax.ShapeDtypeStruct((rows, 2 * len(g) * HD), BF) for g in GROUPS),
        (same, cross), [], 0, 2**21, 8, "pack",
    )


def half_kernel(first, *refs):
    buffers, w = refs[:8], refs[8]
    core, _, z, y = place()
    assemble(w, buffers, first, w.shape[0] // (NZ * NY), core, z, y)


def half_of(buffers, first, rows, name):
    width = buffers[0].shape[1]
    shape = jax.ShapeDtypeStruct((NZ * NY * rows, width), BF)
    return call(
        functools.partial(half_kernel, first), shape, buffers, [], 0, 2**22, 8, name
    )


def attend_frame(scale, q, kv, keep, n):
    rows, keys = q.shape[0], kv.shape[0]
    at, size = n * HD, kv.shape[1] // 2
    score = lax.dot_general(
        q, kv[:, at : at + HD], (((1,), (1,)), ((), ())), preferred_element_type=F32
    )
    weight = jnp.exp2(score * scale).reshape(rows // TILE, TILE, keys)
    weight = jnp.where(keep[:, None, :] > 0, weight, 0.0).reshape(rows, keys).astype(BF)
    value = jnp.concatenate([kv[:, size + at : size + at + HD], jnp.ones((keys, HD), BF)], axis=1)
    return jnp.dot(weight, value, preferred_element_type=F32)


def kept(listed, frame, keys):
    tiles = listed.shape[0]
    lane = lax.div(lax.broadcasted_iota(jnp.int32, (tiles, keys), 1), TILE)
    tile = lane + frame * FRAME
    keep = jnp.zeros((tiles, keys), jnp.bool_)
    for s in range(listed.shape[1]):
        keep = keep | (tile == listed[:, s : s + 1])
    return jnp.where(keep & (tile >= 0), 1.0, 0.0)


def q_kernel(scale, gains, near, w_own, w_other, *refs):
    pieces, kvs = refs[:5], refs[5 : 5 + len(GROUPS)]
    q_ref, acc, w = refs[5 + len(GROUPS) :]
    core, seq, _, _ = place()
    rows = w.shape[0] // (2 * NZ * NY)
    for block in range(NZ * NY):
        span = slice(block * rows, (block + 1) * rows)
        a, b = w_own[span, :], w_other[span, :]
        at = 2 * block * rows
        w[at : at + rows, :] = jnp.where(core == 0, a, b)
        w[at + rows : at + 2 * rows, :] = jnp.where(core == 0, b, a)

    def store(span, product):
        for h in range(product.shape[1] // HD):
            at = slice(h * HD, (h + 1) * HD)
            q_ref[span, at] = normed(product[:, at], gains[0:1, :])

    multiply_tokens(pieces, w, seq, store)
    keep = kept(near[...], lax.axis_index("head"), q_ref.shape[0])
    for kv, group in zip(kvs, GROUPS, strict=True):
        for n, h in enumerate(group):
            acc[h] = attend_frame(scale, q_ref[:, h * HD : (h + 1) * HD], kv, keep, n)


def attend_kernel(scale, group, near, q_ref, acc, before, after, out):
    head = lax.axis_index("head")
    keep = [kept(near[...], head + step, q_ref.shape[0]) for step in (-1, 1)]
    for n, h in enumerate(group):
        q = q_ref[:, h * HD : (h + 1) * HD]
        total = acc[h] + attend_frame(scale, q, before, keep[0], n)
        total = total + attend_frame(scale, q, after, keep[1], n)
        out[:, n * HD : (n + 1) * HD] = (total[:, :HD] / total[:, HD:]).astype(BF)


def output_kernel(group, w_own, w_other, total, *refs):
    pieces, out = refs[:-1], refs[-1]
    core, seq = lax.axis_index("dp"), lax.axis_index("seq")
    width, cols = w_own.shape[0] // NX, w_own.shape[1]
    size = len(group) * HD
    for w, side in ((w_own, core), (w_other, 1 - core)):
        to = pl.ds(pl.multiple_of(side * cols, HD), cols)

        def part(ref, step, w=w):
            at = pl.multiple_of(lax.rem(seq + step, NX) * width + group[0] * HD, HD)
            return jnp.dot(ref[...], w[pl.ds(at, size), :], preferred_element_type=F32)

        near = part(pieces[0], 0) + part(pieces[1], 3) + part(pieces[2], 1)
        if total is not None:
            near = near + total[:, to]
        start = 0
        for far in pieces[3:]:
            rows = slice(start, start + far.shape[0])
            out[rows, to] = (near[rows] + part(far, 2)).astype(out.dtype)
            start += far.shape[0]


def first_kernel(group, w_own, w_other, *refs):
    output_kernel(group, w_own, w_other, None, *refs)


def ring_x(x):
    half = x.shape[0] // 2
    below = along(x, "seq", 1)
    above = along(x, "seq", -1)
    return x, below, above, along(below[:half], "seq", 1), along(above[half:], "seq", -1)


def direct_x(x):
    return x, along(x, "seq", 1), along(x, "seq", -1), along(x, "seq", 2)


def per_device(tokens_in, qkv_weight, norm_gains, out_weight, neighbours):
    rows, feats = tokens_in.shape
    width = qkv_weight.shape[2]
    heads = width // HD
    depth = qkv_weight.shape[0]
    mine = call(
        prepare_kernel,
        jax.ShapeDtypeStruct((depth * 3 // 2 + out_weight.shape[1], width), BF),
        (jnp.transpose(qkv_weight, (1, 0, 2)), jnp.transpose(out_weight)),
        [], 2**35, 2**20, 8, "prepare",
    )
    tokens, others, buffers = gathered(tokens_in, mine)

    kv = project_kv(norm_gains, tokens, others, buffers)
    sides = [[frames_on(x, step) for step in (1, -1)] for x in kv]
    scale = HD ** (-0.5) * math.log2(math.e)
    w_q = half_of(buffers, depth, depth // 2, "query_half")
    query, acc = call(
        functools.partial(q_kernel, scale),
        (
            jax.ShapeDtypeStruct((rows, width), BF),
            jax.ShapeDtypeStruct((heads, rows, 2 * HD), F32),
        ),
        (norm_gains, neighbours, w_q, swapped(w_q), *tokens, *kv),
        [pltpu.VMEM((NX * feats, width), BF)],
        2**35, 6 * 2**20, 20, "query",
    )
    first = depth * 3 // 2
    w_out = half_of(buffers, first, mine.shape[0] - first, "out_half")
    w_outs = (w_out, swapped(w_out))
    total = ()
    for g, group in enumerate(GROUPS):
        last = g == len(GROUPS) - 1
        out = call(
            functools.partial(attend_kernel, scale, group),
            jax.ShapeDtypeStruct((rows, len(group) * HD), BF),
            (neighbours, query, acc, *sides[g]),
            [], (2**35 if not last else 2**30), 4 * 2**20, 16, "attend_%d" % g,
        )
        pieces = (direct_x if last and g else ring_x)(out)
        total = (
            call(
                functools.partial(output_kernel if g else first_kernel, group),
                jax.ShapeDtypeStruct((rows, feats), BF if last else F32),
                (*w_outs, *total, *pieces),
                [], 8 * rows * feats * len(group) * HD, 5 * 2**20, 16, "output_%d" % g,
            ),
        )
    return total[0]


def solution(mesh):
    placed = (
        P(("dp", "head"), "seq"),
        P("head", None, "seq"),
        P(),
        P("seq", "head"),
        P(("dp", "head"), None),
    )
    return jax.shard_map(
        per_device, mesh=mesh, in_specs=placed, out_specs=P(("dp", "head"), "seq"), check_vma=False
    )
```

```python
import functools
import math

import jax
import jax.numpy as jnp
from jax import lax
from jax.experimental import pallas as pl
from jax.experimental.pallas import tpu as pltpu
from jax.sharding import PartitionSpec as P

HD = 128
TILE = 128
FRAME = 4
NX, NY, NZ = 4, 4, 8
BF = jnp.bfloat16
F32 = jnp.float32
VMEM = pl.BlockSpec(memory_space=pltpu.VMEM)

SUB_0 = ((0, 0), (0, -1), (0, 1), (0, 2))
SUB_1 = ((0, 0), (-2, 0), (2, 0), (4, 0))
BUF_0 = ((0, 0), (-1, 0), (1, 0), (-2, 0), (2, 0), (-3, 0), (3, 0), (-4, 0))
BUF_1 = ((0, 0), (1, 0), (0, 1), (1, -1), (0, 2), (1, -2), (0, 3), (1, -3))
GROUPS = ((0, 1), (2,))


def moved(x, core0, core1):
    pairs = []
    for core, (dz, dy) in enumerate((core0, core1)):
        for z in range(NZ):
            for y in range(NY):
                target = ((z + dz) % NZ) * NY + (y + dy) % NY
                pairs.append((core * NZ * NY + z * NY + y, core * NZ * NY + target))
    return lax.ppermute(x, ("dp", "head"), pairs)


def frames_on(x, step, cross):
    n = NZ * NY
    pairs = []
    for core in range(2):
        to = 1 - core if cross else core
        pairs += [(core * n + i, to * n + (i + step) % n) for i in range(n)]
    return lax.ppermute(x, ("dp", "head"), pairs)


def along(x, axis, step):
    n = lax.axis_size(axis)
    return lax.ppermute(x, axis, [(i, (i + step) % n) for i in range(n)])


def swapped(x):
    return lax.ppermute(x, "dp", [(0, 1), (1, 0)])


def halves_kernel(below, above, top, bottom):
    half = top.shape[0]
    top[...] = below[:half, :]
    bottom[...] = above[half:, :]


def halves(below, above):
    shape = jax.ShapeDtypeStruct((below.shape[0] // 2, below.shape[1]), BF)
    return call(halves_kernel, (shape, shape), (below, above), [], 2**34, 2**20, 8, "halves")


def gathered(tokens, mine):
    below = along(tokens, "seq", 1)
    above = along(tokens, "seq", -1)
    a = moved(mine, (0, 1), (2, 0))
    b = moved(mine, (0, -1), (-2, 0))
    c = moved(mine, (0, 2), (4, 0))
    s = jnp.concatenate([mine, a, b, c], axis=0)
    p1 = moved(s, (1, 0), (-1, 0))
    top, bottom = halves(below, above)
    below, above, top, bottom, p1, s = lax.optimization_barrier(
        (below, above, top, bottom, p1, s)
    )
    far_top = along(top, "seq", 1)
    far_bottom = along(bottom, "seq", -1)
    p3, p2 = moved(p1, (1, 0), (0, 1)), moved(s, (-1, 0), (0, -1))
    p5, p4 = moved(p3, (1, 0), (0, 1)), moved(p2, (-1, 0), (0, -1))
    pieces = (tokens, below, above, far_top, far_bottom)
    others = tuple(swapped(x) for x in pieces)
    *others, p5, p4 = lax.optimization_barrier((*others, p5, p4))
    p7, p6 = moved(p5, (1, 0), (0, 1)), moved(p4, (-1, 0), (0, -1))
    return pieces, others, (s, p1, p2, p3, p4, p5, p6, p7)


def prepare_kernel(columns, out_w, mine):
    core = lax.axis_index("dp")
    rows, cols = columns.shape[1:]
    half = rows // 2
    mine[:rows, :] = jnp.where(core == 0, columns[1], columns[2])
    mine[rows : rows + half, :] = jnp.where(core == 0, columns[0, :half, :], columns[0, half:, :])
    mine[rows + half :, :] = jnp.where(core == 0, out_w[:, :cols], out_w[:, cols:])


def place():
    head = lax.axis_index("head")
    return lax.axis_index("dp"), lax.axis_index("seq"), lax.div(head, NY), lax.rem(head, NY)


def block_of(z, y, core, k, i):
    z0, y0 = BUF_0[k][0] + SUB_0[i][0], BUF_0[k][1] + SUB_0[i][1]
    z1, y1 = BUF_1[k][0] + SUB_1[i][0], BUF_1[k][1] + SUB_1[i][1]
    dz = jnp.where(core == 0, z0 % NZ, z1 % NZ)
    dy = jnp.where(core == 0, y0 % NY, y1 % NY)
    return lax.rem(z + dz, NZ) * NY + lax.rem(y + dy, NY)


def normed(values, gain):
    mean_sq = jnp.mean(values * values, axis=-1, keepdims=True)
    return (values * lax.rsqrt(mean_sq + 1e-06) * gain).astype(BF)


def call(kernel, out_shape, args, scratch, flops, nbytes, limit, name):
    n = len(args)
    many = isinstance(out_shape, tuple)
    return pl.pallas_call(
        kernel,
        out_shape=out_shape,
        in_specs=[VMEM] * n,
        out_specs=(VMEM,) * len(out_shape) if many else VMEM,
        scratch_shapes=scratch,
        compiler_params=pltpu.CompilerParams(vmem_limit_bytes=limit * 2**20),
        cost_estimate=pl.CostEstimate(flops=flops, bytes_accessed=nbytes, transcendentals=0),
        name=name,
    )(*args)


def assemble(w, buffers, first, rows, core, z, y):
    size = buffers[0].shape[0] // 4
    for k, ref in enumerate(buffers):
        for i in range(4):
            at = pl.multiple_of(block_of(z, y, core, k, i) * rows, 16)
            start = i * size + first
            w[pl.ds(at, rows), :] = ref[start : start + rows, :]


def multiply_tokens(pieces, w, seq, store):
    own, below, above, far_top, far_bottom = pieces
    feats, half = own.shape[1], far_top.shape[0]

    def part(ref, step):
        at = pl.multiple_of(lax.rem(seq + step, NX) * feats, 128)
        return jnp.dot(ref[...], w[pl.ds(at, feats), :], preferred_element_type=F32)

    near = part(own, 0) + part(below, 3) + part(above, 1)
    store(slice(0, half), near[:half] + part(far_top, 2))
    store(slice(half, 2 * half), near[half:] + part(far_bottom, 2))


def kv_store(outs, core, gains):
    def store(rows, product):
        for out, group in zip(outs, GROUPS, strict=True):
            for n, h in enumerate(group):
                part = product[:, h * HD : (h + 1) * HD]
                out[rows, n * HD : (n + 1) * HD] = jnp.where(
                    core == 0, normed(part, gains[1:2, :]), part.astype(BF)
                )

    return store


def cross_kernel(gains, *refs):
    pieces, buffers = refs[:5], refs[5:13]
    outs, w = refs[13:-1], refs[-1]
    core, seq, z, y = place()
    assemble(w, buffers, 0, w.shape[0] // (NZ * NY), core, z, y)
    multiply_tokens(pieces, w, seq, kv_store(outs, core, gains))


def same_kernel(gains, *refs):
    pieces, w, outs = refs[:5], refs[5], refs[6:]
    core, seq, _, _ = place()
    multiply_tokens(pieces, w, seq, kv_store(outs, core, gains))


def pack_kernel(a, b, out):
    core = lax.axis_index("dp")
    size = a.shape[1]
    out[:, :size] = jnp.where(core == 0, a[...], b[...])
    out[:, size:] = jnp.where(core == 0, b[...], a[...])


def group_shapes(rows):
    return tuple(jax.ShapeDtypeStruct((rows, len(g) * HD), BF) for g in GROUPS)


def project_cross(gains, others, buffers):
    rows, feats = others[0].shape
    depth, width = NX * feats, buffers[0].shape[1]
    return call(
        cross_kernel,
        (*group_shapes(rows), jax.ShapeDtypeStruct((depth, width), BF)),
        (gains, *others, *buffers), [], 2 * rows * depth * width, 6 * 2**20, 20, "project_cross",
    )


def project_same(gains, tokens, w):
    rows, feats = tokens[0].shape
    depth, width = w.shape
    return call(
        same_kernel, group_shapes(rows), (gains, *tokens, w),
        [], 2 * rows * depth * width, 6 * 2**20, 20, "project_same",
    )


def half_kernel(first, *refs):
    buffers, w = refs[:8], refs[8]
    core, _, z, y = place()
    assemble(w, buffers, first, w.shape[0] // (NZ * NY), core, z, y)


def half_of(buffers, first, rows, name):
    width = buffers[0].shape[1]
    shape = jax.ShapeDtypeStruct((NZ * NY * rows, width), BF)
    return call(
        functools.partial(half_kernel, first), shape, buffers, [], 0, 2**22, 8, name
    )


def attend_frame(scale, q, key, value, keep):
    rows, keys = q.shape[0], key.shape[0]
    score = lax.dot_general(q, key, (((1,), (1,)), ((), ())), preferred_element_type=F32)
    weight = jnp.exp2(score * scale).reshape(rows // TILE, TILE, keys)
    weight = jnp.where(keep[:, None, :] > 0, weight, 0.0).reshape(rows, keys).astype(BF)
    value = jnp.concatenate([value, jnp.ones((keys, HD), BF)], axis=1)
    return jnp.dot(weight, value, preferred_element_type=F32)


def picked(a, b, n):
    core = lax.axis_index("dp")
    at = slice(n * HD, (n + 1) * HD)
    return jnp.where(core == 0, a[:, at], b[:, at]), jnp.where(core == 0, b[:, at], a[:, at])


def unpacked(kv, n):
    size = kv.shape[1] // 2
    return kv[:, n * HD : (n + 1) * HD], kv[:, size + n * HD : size + (n + 1) * HD]


def kept(listed, frame, keys):
    tiles = listed.shape[0]
    lane = lax.div(lax.broadcasted_iota(jnp.int32, (tiles, keys), 1), TILE)
    tile = lane + frame * FRAME
    keep = jnp.zeros((tiles, keys), jnp.bool_)
    for s in range(listed.shape[1]):
        keep = keep | (tile == listed[:, s : s + 1])
    return jnp.where(keep & (tile >= 0), 1.0, 0.0)


def q_kernel(gains, w_own, w_other, *refs):
    pieces, q_ref, w = refs[:5], refs[5], refs[6]
    core, seq, _, _ = place()
    rows = w.shape[0] // (2 * NZ * NY)
    for block in range(NZ * NY):
        span = slice(block * rows, (block + 1) * rows)
        a, b = w_own[span, :], w_other[span, :]
        at = 2 * block * rows
        w[at : at + rows, :] = jnp.where(core == 0, a, b)
        w[at + rows : at + 2 * rows, :] = jnp.where(core == 0, b, a)

    def store(span, product):
        for h in range(product.shape[1] // HD):
            at = slice(h * HD, (h + 1) * HD)
            q_ref[span, at] = normed(product[:, at], gains[0:1, :])

    multiply_tokens(pieces, w, seq, store)


def own_kernel(scale, near, q_ref, *refs):
    acc = refs[-1]
    keep = kept(near[...], lax.axis_index("head"), q_ref.shape[0])
    for g, group in enumerate(GROUPS):
        for n, h in enumerate(group):
            key, value = picked(refs[2 * g], refs[2 * g + 1], n)
            acc[h] = attend_frame(scale, q_ref[:, h * HD : (h + 1) * HD], key, value, keep)


def attend_kernel(scale, group, near, q_ref, acc, *refs):
    sides, out = refs[:-1], refs[-1]
    head = lax.axis_index("head")
    keep = [kept(near[...], head + step, q_ref.shape[0]) for step in (-1, 1)]
    for n, h in enumerate(group):
        q = q_ref[:, h * HD : (h + 1) * HD]
        total = acc[h]
        for j in range(2):
            if len(sides) == 4:
                key, value = picked(sides[2 * j], sides[2 * j + 1], n)
            else:
                key, value = unpacked(sides[j], n)
            total = total + attend_frame(scale, q, key, value, keep[j])
        out[:, n * HD : (n + 1) * HD] = (total[:, :HD] / total[:, HD:]).astype(BF)


def output_kernel(group, w_own, w_other, total, *refs):
    pieces, out = refs[:-1], refs[-1]
    core, seq = lax.axis_index("dp"), lax.axis_index("seq")
    width, cols = w_own.shape[0] // NX, w_own.shape[1]
    size = len(group) * HD
    for w, side in ((w_own, core), (w_other, 1 - core)):
        to = pl.ds(pl.multiple_of(side * cols, HD), cols)

        def part(ref, step, w=w):
            at = pl.multiple_of(lax.rem(seq + step, NX) * width + group[0] * HD, HD)
            return jnp.dot(ref[...], w[pl.ds(at, size), :], preferred_element_type=F32)

        near = part(pieces[0], 0) + part(pieces[1], 3) + part(pieces[2], 1)
        if total is not None:
            near = near + total[:, to]
        start = 0
        for far in pieces[3:]:
            rows = slice(start, start + far.shape[0])
            out[rows, to] = (near[rows] + part(far, 2)).astype(out.dtype)
            start += far.shape[0]


def first_kernel(group, w_own, w_other, *refs):
    output_kernel(group, w_own, w_other, None, *refs)


def ring_x(x):
    half = x.shape[0] // 2
    below = along(x, "seq", 1)
    above = along(x, "seq", -1)
    return x, below, above, along(below[:half], "seq", 1), along(above[half:], "seq", -1)


def direct_x(x):
    return x, along(x, "seq", 1), along(x, "seq", -1), along(x, "seq", 2)


def per_device(tokens_in, qkv_weight, norm_gains, out_weight, neighbours):
    rows, feats = tokens_in.shape
    width = qkv_weight.shape[2]
    heads = width // HD
    depth = qkv_weight.shape[0]
    mine = call(
        prepare_kernel,
        jax.ShapeDtypeStruct((depth * 3 // 2 + out_weight.shape[1], width), BF),
        (jnp.transpose(qkv_weight, (1, 0, 2)), jnp.transpose(out_weight)),
        [], 2**35, 2**20, 8, "prepare",
    )
    tokens, others, buffers = gathered(tokens_in, mine)

    w_q = half_of(buffers, depth, depth // 2, "query_half")
    w_q_other = swapped(w_q)
    *cross, w = project_cross(norm_gains, others, buffers)
    others_kv = [swapped(x) for x in cross]
    b0, b1 = (frames_on(cross[0], step, True) for step in (1, -1))
    gains, w, *others_kv = lax.optimization_barrier((norm_gains, w, *others_kv))
    same = project_same(gains, tokens, w)
    a0, a1 = (frames_on(same[0], step, False) for step in (1, -1))
    query = call(
        q_kernel, jax.ShapeDtypeStruct((rows, width), BF),
        (norm_gains, w_q, w_q_other, *tokens),
        [pltpu.VMEM((NX * feats, width), BF)], 2**35, 6 * 2**20, 20, "query",
    )
    late, _ = lax.optimization_barrier((same[1], query))
    packed = call(
        pack_kernel, jax.ShapeDtypeStruct((rows, 2 * late.shape[1]), BF),
        (late, others_kv[1]), [], 0, 2**19, 8, "pack",
    )
    sides = [(a0, b0, a1, b1), tuple(frames_on(packed, step, False) for step in (1, -1))]
    scale = HD ** (-0.5) * math.log2(math.e)
    acc = call(
        functools.partial(own_kernel, scale),
        jax.ShapeDtypeStruct((heads, rows, 2 * HD), F32),
        (neighbours, query, same[0], others_kv[0], same[1], others_kv[1]),
        [], 2**35, 6 * 2**20, 20, "own_frame",
    )
    first = depth * 3 // 2
    w_out = half_of(buffers, first, mine.shape[0] - first, "out_half")
    w_outs = (w_out, swapped(w_out))
    total = ()
    for g, group in enumerate(GROUPS):
        last = g == len(GROUPS) - 1
        out = call(
            functools.partial(attend_kernel, scale, group),
            jax.ShapeDtypeStruct((rows, len(group) * HD), BF),
            (neighbours, query, acc, *sides[g]),
            [], 2**30, 4 * 2**20, 16, "attend_%d" % g,
        )
        pieces = direct_x(out)
        total = (
            call(
                functools.partial(output_kernel if g else first_kernel, group),
                jax.ShapeDtypeStruct((rows, feats), BF if last else F32),
                (*w_outs, *total, *pieces),
                [], 8 * rows * feats * len(group) * HD, 5 * 2**20, 16, "output_%d" % g,
            ),
        )
    return total[0]


def solution(mesh):
    placed = (
        P(("dp", "head"), "seq"),
        P("head", None, "seq"),
        P(),
        P("seq", "head"),
        P(("dp", "head"), None),
    )
    return jax.shard_map(
        per_device, mesh=mesh, in_specs=placed, out_specs=P(("dp", "head"), "seq"), check_vma=False
    )
```

```python
import functools
import math

import jax
import jax.numpy as jnp
from jax import lax
from jax.experimental import pallas as pl
from jax.experimental.pallas import tpu as pltpu
from jax.sharding import PartitionSpec as P

HD = 128
TILE = 128
FRAME = 4
NX, NY, NZ = 4, 4, 8
BF = jnp.bfloat16
F32 = jnp.float32
VMEM = pl.BlockSpec(memory_space=pltpu.VMEM)

SUB_0 = ((0, 0), (0, -1), (0, 1), (0, 2))
SUB_1 = ((0, 0), (-2, 0), (2, 0), (4, 0))
BUF_0 = ((0, 0), (-1, 0), (1, 0), (-2, 0), (2, 0), (-3, 0), (3, 0), (-4, 0))
BUF_1 = ((0, 0), (1, 0), (0, 1), (1, -1), (0, 2), (1, -2), (0, 3), (1, -3))
GROUPS = ((0, 1), (2,))


def moved(x, core0, core1):
    pairs = []
    for core, (dz, dy) in enumerate((core0, core1)):
        for z in range(NZ):
            for y in range(NY):
                target = ((z + dz) % NZ) * NY + (y + dy) % NY
                pairs.append((core * NZ * NY + z * NY + y, core * NZ * NY + target))
    return lax.ppermute(x, ("dp", "head"), pairs)


def frames_on(x, step, cross):
    n = NZ * NY
    pairs = []
    for core in range(2):
        to = 1 - core if cross else core
        pairs += [(core * n + i, to * n + (i + step) % n) for i in range(n)]
    return lax.ppermute(x, ("dp", "head"), pairs)


def along(x, axis, step):
    n = lax.axis_size(axis)
    return lax.ppermute(x, axis, [(i, (i + step) % n) for i in range(n)])


def swapped(x):
    return lax.ppermute(x, "dp", [(0, 1), (1, 0)])


def halves_kernel(below, above, top, bottom):
    half = top.shape[0]
    top[...] = below[:half, :]
    bottom[...] = above[half:, :]


def halves(below, above):
    shape = jax.ShapeDtypeStruct((below.shape[0] // 2, below.shape[1]), BF)
    return call(halves_kernel, (shape, shape), (below, above), [], 2**34, 2**20, 8, "halves")


def gathered(tokens, mine):
    below = along(tokens, "seq", 1)
    above = along(tokens, "seq", -1)
    a = moved(mine, (0, 1), (2, 0))
    b = moved(mine, (0, -1), (-2, 0))
    c = moved(mine, (0, 2), (4, 0))
    s = jnp.concatenate([mine, a, b, c], axis=0)
    p1 = moved(s, (1, 0), (-1, 0))
    top, bottom = halves(below, above)
    below, above, top, bottom, p1, s = lax.optimization_barrier(
        (below, above, top, bottom, p1, s)
    )
    far_top = along(top, "seq", 1)
    far_bottom = along(bottom, "seq", -1)
    p3, p2 = moved(p1, (1, 0), (0, 1)), moved(s, (-1, 0), (0, -1))
    p5, p4 = moved(p3, (1, 0), (0, 1)), moved(p2, (-1, 0), (0, -1))
    pieces = (tokens, below, above, far_top, far_bottom)
    others = [swapped(x) for x in pieces]
    *others[3:], p5, p4 = lax.optimization_barrier((*others[3:], p5, p4))
    p7, p6 = moved(p5, (1, 0), (0, 1)), moved(p4, (-1, 0), (0, -1))
    return pieces, others, (s, p1, p2, p3, p4, p5, p6, p7)


def prepare_kernel(columns, out_w, mine):
    core = lax.axis_index("dp")
    rows, cols = columns.shape[1:]
    half = rows // 2
    mine[:rows, :] = jnp.where(core == 0, columns[1], columns[2])
    mine[rows : rows + half, :] = jnp.where(core == 0, columns[0, :half, :], columns[0, half:, :])
    mine[rows + half :, :] = jnp.where(core == 0, out_w[:, :cols], out_w[:, cols:])


def place():
    head = lax.axis_index("head")
    return lax.axis_index("dp"), lax.axis_index("seq"), lax.div(head, NY), lax.rem(head, NY)


def block_of(z, y, core, k, i):
    z0, y0 = BUF_0[k][0] + SUB_0[i][0], BUF_0[k][1] + SUB_0[i][1]
    z1, y1 = BUF_1[k][0] + SUB_1[i][0], BUF_1[k][1] + SUB_1[i][1]
    dz = jnp.where(core == 0, z0 % NZ, z1 % NZ)
    dy = jnp.where(core == 0, y0 % NY, y1 % NY)
    return lax.rem(z + dz, NZ) * NY + lax.rem(y + dy, NY)


def normed(values, gain):
    mean_sq = jnp.mean(values * values, axis=-1, keepdims=True)
    return (values * lax.rsqrt(mean_sq + 1e-06) * gain).astype(BF)


def call(kernel, out_shape, args, scratch, flops, nbytes, limit, name):
    n = len(args)
    many = isinstance(out_shape, tuple)
    return pl.pallas_call(
        kernel,
        out_shape=out_shape,
        in_specs=[VMEM] * n,
        out_specs=(VMEM,) * len(out_shape) if many else VMEM,
        scratch_shapes=scratch,
        compiler_params=pltpu.CompilerParams(vmem_limit_bytes=limit * 2**20),
        cost_estimate=pl.CostEstimate(flops=flops, bytes_accessed=nbytes, transcendentals=0),
        name=name,
    )(*args)


def assemble(w, buffers, first, rows, core, z, y):
    size = buffers[0].shape[0] // 4
    for k, ref in enumerate(buffers):
        for i in range(4):
            at = pl.multiple_of(block_of(z, y, core, k, i) * rows, 16)
            start = i * size + first
            w[pl.ds(at, rows), :] = ref[start : start + rows, :]


def multiply_tokens(pieces, w, seq, store):
    own, below, above, far_top, far_bottom = pieces
    feats, half = own.shape[1], far_top.shape[0]

    def part(ref, step):
        at = pl.multiple_of(lax.rem(seq + step, NX) * feats, 128)
        return jnp.dot(ref[...], w[pl.ds(at, feats), :], preferred_element_type=F32)

    near = part(own, 0) + part(below, 3) + part(above, 1)
    store(slice(0, half), near[:half] + part(far_top, 2))
    store(slice(half, 2 * half), near[half:] + part(far_bottom, 2))


def kv_store(outs, core, gains):
    def store(rows, product):
        for out, group in zip(outs, GROUPS, strict=True):
            for n, h in enumerate(group):
                part = product[:, h * HD : (h + 1) * HD]
                out[rows, n * HD : (n + 1) * HD] = jnp.where(
                    core == 0, normed(part, gains[1:2, :]), part.astype(BF)
                )

    return store


def cross_kernel(gains, *refs):
    pieces, buffers = refs[:5], refs[5:13]
    outs, w = refs[13:-1], refs[-1]
    core, seq, z, y = place()
    assemble(w, buffers, 0, w.shape[0] // (NZ * NY), core, z, y)
    multiply_tokens(pieces, w, seq, kv_store(outs, core, gains))


def same_kernel(gains, *refs):
    pieces, w, outs = refs[:5], refs[5], refs[6:]
    core, seq, _, _ = place()
    multiply_tokens(pieces, w, seq, kv_store(outs, core, gains))


def pack_kernel(a, b, out):
    core = lax.axis_index("dp")
    size = a.shape[1]
    out[:, :size] = jnp.where(core == 0, a[...], b[...])
    out[:, size:] = jnp.where(core == 0, b[...], a[...])


def group_shapes(rows):
    return tuple(jax.ShapeDtypeStruct((rows, len(g) * HD), BF) for g in GROUPS)


def project_cross(gains, others, buffers):
    rows, feats = others[0].shape
    depth, width = NX * feats, buffers[0].shape[1]
    return call(
        cross_kernel,
        (*group_shapes(rows), jax.ShapeDtypeStruct((depth, width), BF)),
        (gains, *others, *buffers), [], 2 * rows * depth * width, 6 * 2**20, 20, "project_cross",
    )


def project_same(gains, tokens, w):
    rows, feats = tokens[0].shape
    depth, width = w.shape
    return call(
        same_kernel, group_shapes(rows), (gains, *tokens, w),
        [], 2 * rows * depth * width, 6 * 2**20, 20, "project_same",
    )


def half_kernel(first, *refs):
    buffers, w = refs[:8], refs[8]
    core, _, z, y = place()
    assemble(w, buffers, first, w.shape[0] // (NZ * NY), core, z, y)


def half_of(buffers, first, rows, name):
    width = buffers[0].shape[1]
    shape = jax.ShapeDtypeStruct((NZ * NY * rows, width), BF)
    return call(
        functools.partial(half_kernel, first), shape, buffers, [], 0, 2**22, 8, name
    )


def attend_frame(scale, q, key, value, keep):
    rows, keys = q.shape[0], key.shape[0]
    score = lax.dot_general(q, key, (((1,), (1,)), ((), ())), preferred_element_type=F32)
    weight = jnp.exp2(score * scale).reshape(rows // TILE, TILE, keys)
    weight = jnp.where(keep[:, None, :] > 0, weight, 0.0).reshape(rows, keys).astype(BF)
    value = jnp.concatenate([value, jnp.ones((keys, HD), BF)], axis=1)
    return jnp.dot(weight, value, preferred_element_type=F32)


def picked(a, b, n):
    core = lax.axis_index("dp")
    at = slice(n * HD, (n + 1) * HD)
    return jnp.where(core == 0, a[:, at], b[:, at]), jnp.where(core == 0, b[:, at], a[:, at])


def unpacked(kv, n):
    size = kv.shape[1] // 2
    return kv[:, n * HD : (n + 1) * HD], kv[:, size + n * HD : size + (n + 1) * HD]


def kept(listed, frame, keys):
    tiles = listed.shape[0]
    lane = lax.div(lax.broadcasted_iota(jnp.int32, (tiles, keys), 1), TILE)
    tile = lane + frame * FRAME
    keep = jnp.zeros((tiles, keys), jnp.bool_)
    for s in range(listed.shape[1]):
        keep = keep | (tile == listed[:, s : s + 1])
    return jnp.where(keep & (tile >= 0), 1.0, 0.0)


def q_kernel(gains, w_own, w_other, *refs):
    pieces, q_ref, w = refs[:5], refs[5], refs[6]
    core, seq, _, _ = place()
    rows = w.shape[0] // (2 * NZ * NY)
    for block in range(NZ * NY):
        span = slice(block * rows, (block + 1) * rows)
        a, b = w_own[span, :], w_other[span, :]
        at = 2 * block * rows
        w[at : at + rows, :] = jnp.where(core == 0, a, b)
        w[at + rows : at + 2 * rows, :] = jnp.where(core == 0, b, a)

    def store(span, product):
        for h in range(product.shape[1] // HD):
            at = slice(h * HD, (h + 1) * HD)
            q_ref[span, at] = normed(product[:, at], gains[0:1, :])

    multiply_tokens(pieces, w, seq, store)


def own_kernel(scale, near, q_ref, *refs):
    acc = refs[-1]
    keep = kept(near[...], lax.axis_index("head"), q_ref.shape[0])
    for g, group in enumerate(GROUPS):
        for n, h in enumerate(group):
            key, value = picked(refs[2 * g], refs[2 * g + 1], n)
            acc[h] = attend_frame(scale, q_ref[:, h * HD : (h + 1) * HD], key, value, keep)


def attend_kernel(scale, group, near, q_ref, acc, *refs):
    sides, out = refs[:-1], refs[-1]
    head = lax.axis_index("head")
    keep = [kept(near[...], head + step, q_ref.shape[0]) for step in (-1, 1)]
    for n, h in enumerate(group):
        q = q_ref[:, h * HD : (h + 1) * HD]
        total = acc[h]
        for j in range(2):
            if len(sides) == 4:
                key, value = picked(sides[2 * j], sides[2 * j + 1], n)
            else:
                key, value = unpacked(sides[j], n)
            total = total + attend_frame(scale, q, key, value, keep[j])
        out[:, n * HD : (n + 1) * HD] = (total[:, :HD] / total[:, HD:]).astype(BF)


def output_kernel(group, w_own, w_other, total, *refs):
    pieces, out = refs[:-1], refs[-1]
    core, seq = lax.axis_index("dp"), lax.axis_index("seq")
    width, cols = w_own.shape[0] // NX, w_own.shape[1]
    size = len(group) * HD
    pairs = [
        (jnp.concatenate([pieces[i][...], pieces[j][...]], axis=1), (steps_i, steps_j))
        for (i, steps_i), (j, steps_j) in (((0, 0), (1, 3)), ((2, 1), (3, 2)))
    ]
    for w, side in ((w_own, core), (w_other, 1 - core)):
        to = pl.ds(pl.multiple_of(side * cols, HD), cols)
        product = None if total is None else total[:, to]
        for x, steps in pairs:
            rows = []
            for step in steps:
                at = pl.multiple_of(lax.rem(seq + step, NX) * width + group[0] * HD, HD)
                rows.append(w[pl.ds(at, size), :])
            part = jnp.dot(x, jnp.concatenate(rows, axis=0), preferred_element_type=F32)
            product = part if product is None else product + part
        out[:, to] = product.astype(out.dtype)


def first_kernel(group, w_own, w_other, *refs):
    output_kernel(group, w_own, w_other, None, *refs)


def direct_x(x):
    return x, along(x, "seq", 1), along(x, "seq", -1), along(x, "seq", 2)


def per_device(tokens_in, qkv_weight, norm_gains, out_weight, neighbours):
    rows, feats = tokens_in.shape
    width = qkv_weight.shape[2]
    heads = width // HD
    depth = qkv_weight.shape[0]
    mine = call(
        prepare_kernel,
        jax.ShapeDtypeStruct((depth * 3 // 2 + out_weight.shape[1], width), BF),
        (jnp.transpose(qkv_weight, (1, 0, 2)), jnp.transpose(out_weight)),
        [], 2**35, 2**20, 8, "prepare",
    )
    tokens, others, buffers = gathered(tokens_in, mine)

    w_q = half_of(buffers, depth, depth // 2, "query_half")
    w_q_other = swapped(w_q)
    *cross, w = project_cross(norm_gains, others, buffers)
    others_kv = [swapped(x) for x in cross]
    b0, b1 = (frames_on(cross[0], step, True) for step in (1, -1))
    gains, w, *others_kv = lax.optimization_barrier((norm_gains, w, *others_kv))
    same = project_same(gains, tokens, w)
    a0, a1 = (frames_on(same[0], step, False) for step in (1, -1))
    query = call(
        q_kernel, jax.ShapeDtypeStruct((rows, width), BF),
        (norm_gains, w_q, w_q_other, *tokens),
        [pltpu.VMEM((NX * feats, width), BF)], 2**35, 6 * 2**20, 20, "query",
    )
    late, _ = lax.optimization_barrier((same[1], query))
    packed = call(
        pack_kernel, jax.ShapeDtypeStruct((rows, 2 * late.shape[1]), BF),
        (late, others_kv[1]), [], 0, 2**19, 8, "pack",
    )
    sides = [(a0, b0, a1, b1), tuple(frames_on(packed, step, False) for step in (1, -1))]
    scale = HD ** (-0.5) * math.log2(math.e)
    acc = call(
        functools.partial(own_kernel, scale),
        jax.ShapeDtypeStruct((heads, rows, 2 * HD), F32),
        (neighbours, query, same[0], others_kv[0], same[1], others_kv[1]),
        [], 2**35, 6 * 2**20, 20, "own_frame",
    )
    first = depth * 3 // 2
    w_out = half_of(buffers, first, mine.shape[0] - first, "out_half")
    w_outs = (w_out, swapped(w_out))
    total = ()
    for g, group in enumerate(GROUPS):
        last = g == len(GROUPS) - 1
        out = call(
            functools.partial(attend_kernel, scale, group),
            jax.ShapeDtypeStruct((rows, len(group) * HD), BF),
            (neighbours, query, acc, *sides[g]),
            [], 2**30, 4 * 2**20, 16, "attend_%d" % g,
        )
        pieces = direct_x(out)
        total = (
            call(
                functools.partial(output_kernel if g else first_kernel, group),
                jax.ShapeDtypeStruct((rows, feats), BF if last else F32),
                (*w_outs, *total, *pieces),
                [], 8 * rows * feats * len(group) * HD, 5 * 2**20, 16, "output_%d" % g,
            ),
        )
    return total[0]


def solution(mesh):
    placed = (
        P(("dp", "head"), "seq"),
        P("head", None, "seq"),
        P(),
        P("seq", "head"),
        P(("dp", "head"), None),
    )
    return jax.shard_map(
        per_device, mesh=mesh, in_specs=placed, out_specs=P(("dp", "head"), "seq"), check_vma=False
    )
```

```python
import functools
import math

import jax
import jax.numpy as jnp
from jax import lax
from jax.experimental import pallas as pl
from jax.experimental.pallas import tpu as pltpu
from jax.sharding import PartitionSpec as P

HD = 128
TILE = 128
FRAME = 4
NX, NY, NZ = 4, 4, 8
BF = jnp.bfloat16
F32 = jnp.float32
VMEM = pl.BlockSpec(memory_space=pltpu.VMEM)

SUB_0 = ((0, 0), (0, -1), (0, 1), (0, 2))
SUB_1 = ((0, 0), (-2, 0), (2, 0), (4, 0))
BUF_0 = ((0, 0), (-1, 0), (1, 0), (-2, 0), (2, 0), (-3, 0), (3, 0), (-4, 0))
BUF_1 = ((0, 0), (1, 0), (0, 1), (1, -1), (0, 2), (1, -2), (0, 3), (1, -3))
GROUPS = ((0, 1), (2,))


def moved(x, core0, core1):
    pairs = []
    for core, (dz, dy) in enumerate((core0, core1)):
        for z in range(NZ):
            for y in range(NY):
                target = ((z + dz) % NZ) * NY + (y + dy) % NY
                pairs.append((core * NZ * NY + z * NY + y, core * NZ * NY + target))
    return lax.ppermute(x, ("dp", "head"), pairs)


def frames_on(x, step, cross):
    n = NZ * NY
    pairs = []
    for core in range(2):
        to = 1 - core if cross else core
        pairs += [(core * n + i, to * n + (i + step) % n) for i in range(n)]
    return lax.ppermute(x, ("dp", "head"), pairs)


def along(x, axis, step):
    n = lax.axis_size(axis)
    return lax.ppermute(x, axis, [(i, (i + step) % n) for i in range(n)])


def swapped(x):
    return lax.ppermute(x, "dp", [(0, 1), (1, 0)])


def halves_kernel(below, above, top, bottom):
    half = top.shape[0]
    top[...] = below[:half, :]
    bottom[...] = above[half:, :]


def halves(below, above):
    shape = jax.ShapeDtypeStruct((below.shape[0] // 2, below.shape[1]), BF)
    return call(halves_kernel, (shape, shape), (below, above), [], 2**34, 2**20, 8, "halves")


def gathered(tokens, mine):
    below = along(tokens, "seq", 1)
    above = along(tokens, "seq", -1)
    a = moved(mine, (0, 1), (2, 0))
    b = moved(mine, (0, -1), (-2, 0))
    c = moved(mine, (0, 2), (4, 0))
    s = jnp.concatenate([mine, a, b, c], axis=0)
    p1 = moved(s, (1, 0), (-1, 0))
    top, bottom = halves(below, above)
    below, above, top, bottom, p1, s = lax.optimization_barrier(
        (below, above, top, bottom, p1, s)
    )
    far_top = along(top, "seq", 1)
    far_bottom = along(bottom, "seq", -1)
    p3, p2 = moved(p1, (1, 0), (0, 1)), moved(s, (-1, 0), (0, -1))
    p5, p4 = moved(p3, (1, 0), (0, 1)), moved(p2, (-1, 0), (0, -1))
    pieces = (tokens, below, above, far_top, far_bottom)
    others = [swapped(x) for x in pieces]
    others[3], p5 = lax.optimization_barrier((others[3], p5))
    others[4], p4 = lax.optimization_barrier((others[4], p4))
    p7, p6 = moved(p5, (1, 0), (0, 1)), moved(p4, (-1, 0), (0, -1))
    return pieces, others, (s, p1, p2, p3, p4, p5, p6, p7)


def prepare_kernel(columns, out_w, mine):
    core = lax.axis_index("dp")
    rows, cols = columns.shape[1:]
    half = rows // 2
    mine[:rows, :] = jnp.where(core == 0, columns[1], columns[2])
    mine[rows : rows + half, :] = jnp.where(core == 0, columns[0, :half, :], columns[0, half:, :])
    mine[rows + half :, :] = jnp.where(core == 0, out_w[:, :cols], out_w[:, cols:])


def place():
    head = lax.axis_index("head")
    return lax.axis_index("dp"), lax.axis_index("seq"), lax.div(head, NY), lax.rem(head, NY)


def block_of(z, y, core, k, i):
    z0, y0 = BUF_0[k][0] + SUB_0[i][0], BUF_0[k][1] + SUB_0[i][1]
    z1, y1 = BUF_1[k][0] + SUB_1[i][0], BUF_1[k][1] + SUB_1[i][1]
    dz = jnp.where(core == 0, z0 % NZ, z1 % NZ)
    dy = jnp.where(core == 0, y0 % NY, y1 % NY)
    return lax.rem(z + dz, NZ) * NY + lax.rem(y + dy, NY)


def normed(values, gain):
    mean_sq = jnp.mean(values * values, axis=-1, keepdims=True)
    return (values * lax.rsqrt(mean_sq + 1e-06) * gain).astype(BF)


def call(kernel, out_shape, args, scratch, flops, nbytes, limit, name):
    n = len(args)
    many = isinstance(out_shape, tuple)
    return pl.pallas_call(
        kernel,
        out_shape=out_shape,
        in_specs=[VMEM] * n,
        out_specs=(VMEM,) * len(out_shape) if many else VMEM,
        scratch_shapes=scratch,
        compiler_params=pltpu.CompilerParams(vmem_limit_bytes=limit * 2**20),
        cost_estimate=pl.CostEstimate(flops=flops, bytes_accessed=nbytes, transcendentals=0),
        name=name,
    )(*args)


def assemble(w, buffers, first, rows, core, z, y):
    size = buffers[0].shape[0] // 4
    for k, ref in enumerate(buffers):
        for i in range(4):
            at = pl.multiple_of(block_of(z, y, core, k, i) * rows, 16)
            start = i * size + first
            w[pl.ds(at, rows), :] = ref[start : start + rows, :]


def multiply_tokens(pieces, w, seq, store):
    own, below, above, far_top, far_bottom = pieces
    feats, half = own.shape[1], far_top.shape[0]

    def part(ref, step):
        at = pl.multiple_of(lax.rem(seq + step, NX) * feats, 128)
        return jnp.dot(ref[...], w[pl.ds(at, feats), :], preferred_element_type=F32)

    near = part(own, 0) + part(below, 3) + part(above, 1)
    store(slice(0, half), near[:half] + part(far_top, 2))
    store(slice(half, 2 * half), near[half:] + part(far_bottom, 2))


def kv_store(outs, core, gains):
    def store(rows, product):
        for out, group in zip(outs, GROUPS, strict=True):
            for n, h in enumerate(group):
                part = product[:, h * HD : (h + 1) * HD]
                out[rows, n * HD : (n + 1) * HD] = jnp.where(
                    core == 0, normed(part, gains[1:2, :]), part.astype(BF)
                )

    return store


def cross_kernel(gains, *refs):
    pieces, buffers = refs[:5], refs[5:13]
    outs, w = refs[13:-1], refs[-1]
    core, seq, z, y = place()
    assemble(w, buffers, 0, w.shape[0] // (NZ * NY), core, z, y)
    multiply_tokens(pieces, w, seq, kv_store(outs, core, gains))


def same_kernel(gains, *refs):
    pieces, w, outs = refs[:5], refs[5], refs[6:]
    core, seq, _, _ = place()
    multiply_tokens(pieces, w, seq, kv_store(outs, core, gains))


def pack_kernel(a, b, out):
    core = lax.axis_index("dp")
    size = a.shape[1]
    out[:, :size] = jnp.where(core == 0, a[...], b[...])
    out[:, size:] = jnp.where(core == 0, b[...], a[...])


def group_shapes(rows):
    return tuple(jax.ShapeDtypeStruct((rows, len(g) * HD), BF) for g in GROUPS)


def project_cross(gains, others, buffers):
    rows, feats = others[0].shape
    depth, width = NX * feats, buffers[0].shape[1]
    return call(
        cross_kernel,
        (*group_shapes(rows), jax.ShapeDtypeStruct((depth, width), BF)),
        (gains, *others, *buffers), [], 2 * rows * depth * width, 6 * 2**20, 20, "project_cross",
    )


def project_same(gains, tokens, w):
    rows, feats = tokens[0].shape
    depth, width = w.shape
    return call(
        same_kernel, group_shapes(rows), (gains, *tokens, w),
        [], 2 * rows * depth * width, 6 * 2**20, 20, "project_same",
    )


def half_kernel(first, *refs):
    buffers, w = refs[:8], refs[8]
    core, _, z, y = place()
    assemble(w, buffers, first, w.shape[0] // (NZ * NY), core, z, y)


def half_of(buffers, first, rows, name):
    width = buffers[0].shape[1]
    shape = jax.ShapeDtypeStruct((NZ * NY * rows, width), BF)
    return call(
        functools.partial(half_kernel, first), shape, buffers, [], 0, 2**22, 8, name
    )


def attend_frame(scale, q, key, value, keep):
    rows, keys = q.shape[0], key.shape[0]
    score = lax.dot_general(q, key, (((1,), (1,)), ((), ())), preferred_element_type=F32)
    weight = jnp.exp2(score * scale).reshape(rows // TILE, TILE, keys)
    weight = jnp.where(keep[:, None, :] > 0, weight, 0.0).reshape(rows, keys).astype(BF)
    value = jnp.concatenate([value, jnp.ones((keys, HD), BF)], axis=1)
    return jnp.dot(weight, value, preferred_element_type=F32)


def picked(a, b, n):
    core = lax.axis_index("dp")
    at = slice(n * HD, (n + 1) * HD)
    return jnp.where(core == 0, a[:, at], b[:, at]), jnp.where(core == 0, b[:, at], a[:, at])


def unpacked(kv, n):
    size = kv.shape[1] // 2
    return kv[:, n * HD : (n + 1) * HD], kv[:, size + n * HD : size + (n + 1) * HD]


def kept(listed, frame, keys):
    tiles = listed.shape[0]
    lane = lax.div(lax.broadcasted_iota(jnp.int32, (tiles, keys), 1), TILE)
    tile = lane + frame * FRAME
    keep = jnp.zeros((tiles, keys), jnp.bool_)
    for s in range(listed.shape[1]):
        keep = keep | (tile == listed[:, s : s + 1])
    return jnp.where(keep & (tile >= 0), 1.0, 0.0)


def q_kernel(gains, w_own, w_other, *refs):
    pieces, q_ref, w = refs[:5], refs[5], refs[6]
    core, seq, _, _ = place()
    rows = w.shape[0] // (2 * NZ * NY)
    for block in range(NZ * NY):
        span = slice(block * rows, (block + 1) * rows)
        a, b = w_own[span, :], w_other[span, :]
        at = 2 * block * rows
        w[at : at + rows, :] = jnp.where(core == 0, a, b)
        w[at + rows : at + 2 * rows, :] = jnp.where(core == 0, b, a)

    def store(span, product):
        for h in range(product.shape[1] // HD):
            at = slice(h * HD, (h + 1) * HD)
            q_ref[span, at] = normed(product[:, at], gains[0:1, :])

    multiply_tokens(pieces, w, seq, store)


def own_kernel(scale, near, q_ref, *refs):
    acc = refs[-1]
    keep = kept(near[...], lax.axis_index("head"), q_ref.shape[0])
    for g, group in enumerate(GROUPS):
        for n, h in enumerate(group):
            key, value = picked(refs[2 * g], refs[2 * g + 1], n)
            acc[h] = attend_frame(scale, q_ref[:, h * HD : (h + 1) * HD], key, value, keep)


def attend_kernel(scale, group, near, q_ref, acc, *refs):
    sides, out = refs[:-1], refs[-1]
    head = lax.axis_index("head")
    keep = [kept(near[...], head + step, q_ref.shape[0]) for step in (-1, 1)]
    for n, h in enumerate(group):
        q = q_ref[:, h * HD : (h + 1) * HD]
        total = acc[h]
        for j in range(2):
            if len(sides) == 4:
                key, value = picked(sides[2 * j], sides[2 * j + 1], n)
            else:
                key, value = unpacked(sides[j], n)
            total = total + attend_frame(scale, q, key, value, keep[j])
        out[:, n * HD : (n + 1) * HD] = (total[:, :HD] / total[:, HD:]).astype(BF)


def output_kernel(group, w_own, w_other, total, *refs):
    pieces, out = refs[:-1], refs[-1]
    core, seq = lax.axis_index("dp"), lax.axis_index("seq")
    width, cols = w_own.shape[0] // NX, w_own.shape[1]
    size = len(group) * HD
    pairs = [
        (jnp.concatenate([pieces[i][...], pieces[j][...]], axis=1), (steps_i, steps_j))
        for (i, steps_i), (j, steps_j) in (((0, 0), (1, 3)), ((2, 1), (3, 2)))
    ]
    for w, side in ((w_own, core), (w_other, 1 - core)):
        to = pl.ds(pl.multiple_of(side * cols, HD), cols)
        product = None if total is None else total[:, to]
        for x, steps in pairs:
            rows = []
            for step in steps:
                at = pl.multiple_of(lax.rem(seq + step, NX) * width + group[0] * HD, HD)
                rows.append(w[pl.ds(at, size), :])
            part = jnp.dot(x, jnp.concatenate(rows, axis=0), preferred_element_type=F32)
            product = part if product is None else product + part
        out[:, to] = product.astype(out.dtype)


def first_kernel(group, w_own, w_other, *refs):
    output_kernel(group, w_own, w_other, None, *refs)


def direct_x(x):
    return x, along(x, "seq", 1), along(x, "seq", -1), along(x, "seq", 2)


def per_device(tokens_in, qkv_weight, norm_gains, out_weight, neighbours):
    rows, feats = tokens_in.shape
    width = qkv_weight.shape[2]
    heads = width // HD
    depth = qkv_weight.shape[0]
    mine = call(
        prepare_kernel,
        jax.ShapeDtypeStruct((depth * 3 // 2 + out_weight.shape[1], width), BF),
        (jnp.transpose(qkv_weight, (1, 0, 2)), jnp.transpose(out_weight)),
        [], 2**35, 2**20, 8, "prepare",
    )
    tokens, others, buffers = gathered(tokens_in, mine)

    w_q = half_of(buffers, depth, depth // 2, "query_half")
    w_q_other = swapped(w_q)
    *cross, w = project_cross(norm_gains, others, buffers)
    others_kv = [swapped(x) for x in cross]
    b0, b1 = (frames_on(cross[0], step, True) for step in (1, -1))
    gains, w, *others_kv = lax.optimization_barrier((norm_gains, w, *others_kv))
    same = project_same(gains, tokens, w)
    a0, a1 = (frames_on(same[0], step, False) for step in (1, -1))
    query = call(
        q_kernel, jax.ShapeDtypeStruct((rows, width), BF),
        (norm_gains, w_q, w_q_other, *tokens),
        [pltpu.VMEM((NX * feats, width), BF)], 2**35, 6 * 2**20, 20, "query",
    )
    scale = HD ** (-0.5) * math.log2(math.e)
    acc = call(
        functools.partial(own_kernel, scale),
        jax.ShapeDtypeStruct((heads, rows, 2 * HD), F32),
        (neighbours, query, same[0], others_kv[0], same[1], others_kv[1]),
        [], 2**35, 6 * 2**20, 20, "own_frame",
    )
    late, _ = lax.optimization_barrier((same[1], acc))
    packed = call(
        pack_kernel, jax.ShapeDtypeStruct((rows, 2 * late.shape[1]), BF),
        (late, others_kv[1]), [], 0, 2**19, 8, "pack",
    )
    sides = [(a0, b0, a1, b1), tuple(frames_on(packed, step, False) for step in (1, -1))]
    first = depth * 3 // 2
    w_out = half_of(buffers, first, mine.shape[0] - first, "out_half")
    w_outs = (w_out, swapped(w_out))
    total = ()
    for g, group in enumerate(GROUPS):
        last = g == len(GROUPS) - 1
        out = call(
            functools.partial(attend_kernel, scale, group),
            jax.ShapeDtypeStruct((rows, len(group) * HD), BF),
            (neighbours, query, acc, *sides[g]),
            [], 2**30, 4 * 2**20, 16, "attend_%d" % g,
        )
        pieces = direct_x(out)
        total = (
            call(
                functools.partial(output_kernel if g else first_kernel, group),
                jax.ShapeDtypeStruct((rows, feats), BF if last else F32),
                (*w_outs, *total, *pieces),
                [], 8 * rows * feats * len(group) * HD, 5 * 2**20, 16, "output_%d" % g,
            ),
        )
    return total[0]


def solution(mesh):
    placed = (
        P(("dp", "head"), "seq"),
        P("head", None, "seq"),
        P(),
        P("seq", "head"),
        P(("dp", "head"), None),
    )
    return jax.shard_map(
        per_device, mesh=mesh, in_specs=placed, out_specs=P(("dp", "head"), "seq"), check_vma=False
    )
```

```python
import functools
import math

import jax
import jax.numpy as jnp
from jax import lax
from jax.experimental import pallas as pl
from jax.experimental.pallas import tpu as pltpu
from jax.sharding import PartitionSpec as P

HD = 128
TILE = 128
FRAME = 4
NX, NY, NZ = 4, 4, 8
BF = jnp.bfloat16
F32 = jnp.float32
VMEM = pl.BlockSpec(memory_space=pltpu.VMEM)

SUB_0 = ((0, 0), (0, -1), (0, 1), (0, 2))
SUB_1 = ((0, 0), (-2, 0), (2, 0), (4, 0))
BUF_0 = ((0, 0), (-1, 0), (1, 0), (-2, 0), (2, 0), (-3, 0), (3, 0), (-4, 0))
BUF_1 = ((0, 0), (1, 0), (0, 1), (1, -1), (0, 2), (1, -2), (0, 3), (1, -3))
GROUPS = ((0, 1), (2,))


def moved(x, core0, core1):
    pairs = []
    for core, (dz, dy) in enumerate((core0, core1)):
        for z in range(NZ):
            for y in range(NY):
                target = ((z + dz) % NZ) * NY + (y + dy) % NY
                pairs.append((core * NZ * NY + z * NY + y, core * NZ * NY + target))
    return lax.ppermute(x, ("dp", "head"), pairs)


def frames_on(x, step, cross):
    n = NZ * NY
    pairs = []
    for core in range(2):
        to = 1 - core if cross else core
        pairs += [(core * n + i, to * n + (i + step) % n) for i in range(n)]
    return lax.ppermute(x, ("dp", "head"), pairs)


def along(x, axis, step):
    n = lax.axis_size(axis)
    return lax.ppermute(x, axis, [(i, (i + step) % n) for i in range(n)])


def swapped(x):
    return lax.ppermute(x, "dp", [(0, 1), (1, 0)])


def halves_kernel(below, above, top, bottom):
    half = top.shape[0]
    top[...] = below[:half, :]
    bottom[...] = above[half:, :]


def halves(below, above):
    shape = jax.ShapeDtypeStruct((below.shape[0] // 2, below.shape[1]), BF)
    return call(halves_kernel, (shape, shape), (below, above), [], 2**34, 2**20, 8, "halves")


def gathered(tokens, mine):
    below = along(tokens, "seq", 1)
    above = along(tokens, "seq", -1)
    a = moved(mine, (0, 1), (2, 0))
    b = moved(mine, (0, -1), (-2, 0))
    c = moved(mine, (0, 2), (4, 0))
    s = jnp.concatenate([mine, a, b, c], axis=0)
    p1 = moved(s, (1, 0), (-1, 0))
    top, bottom = halves(below, above)
    below, above, top, bottom, p1, s = lax.optimization_barrier(
        (below, above, top, bottom, p1, s)
    )
    far_top = along(top, "seq", 1)
    far_bottom = along(bottom, "seq", -1)
    p3, p2 = moved(p1, (1, 0), (0, 1)), moved(s, (-1, 0), (0, -1))
    p5, p4 = moved(p3, (1, 0), (0, 1)), moved(p2, (-1, 0), (0, -1))
    pieces = (tokens, below, above, far_top, far_bottom)
    others = [swapped(x) for x in pieces]
    others[3], p5 = lax.optimization_barrier((others[3], p5))
    others[4], p4 = lax.optimization_barrier((others[4], p4))
    p7, p6 = moved(p5, (1, 0), (0, 1)), moved(p4, (-1, 0), (0, -1))
    return pieces, others, (s, p1, p2, p3, p4, p5, p6, p7)


def prepare_kernel(columns, out_w, mine):
    core = lax.axis_index("dp")
    rows, cols = columns.shape[1:]
    half = rows // 2
    mine[:rows, :] = jnp.where(core == 0, columns[1], columns[2])
    mine[rows : rows + half, :] = jnp.where(core == 0, columns[0, :half, :], columns[0, half:, :])
    mine[rows + half :, :] = jnp.where(core == 0, out_w[:, :cols], out_w[:, cols:])


def place():
    head = lax.axis_index("head")
    return lax.axis_index("dp"), lax.axis_index("seq"), lax.div(head, NY), lax.rem(head, NY)


def block_of(z, y, core, k, i):
    z0, y0 = BUF_0[k][0] + SUB_0[i][0], BUF_0[k][1] + SUB_0[i][1]
    z1, y1 = BUF_1[k][0] + SUB_1[i][0], BUF_1[k][1] + SUB_1[i][1]
    dz = jnp.where(core == 0, z0 % NZ, z1 % NZ)
    dy = jnp.where(core == 0, y0 % NY, y1 % NY)
    return lax.rem(z + dz, NZ) * NY + lax.rem(y + dy, NY)


def normed(values, gain):
    mean_sq = jnp.mean(values * values, axis=-1, keepdims=True)
    return (values * lax.rsqrt(mean_sq + 1e-06) * gain).astype(BF)


def call(kernel, out_shape, args, scratch, flops, nbytes, limit, name):
    n = len(args)
    many = isinstance(out_shape, tuple)
    return pl.pallas_call(
        kernel,
        out_shape=out_shape,
        in_specs=[VMEM] * n,
        out_specs=(VMEM,) * len(out_shape) if many else VMEM,
        scratch_shapes=scratch,
        compiler_params=pltpu.CompilerParams(vmem_limit_bytes=limit * 2**20),
        cost_estimate=pl.CostEstimate(flops=flops, bytes_accessed=nbytes, transcendentals=0),
        name=name,
    )(*args)


def assemble(w, buffers, first, rows, core, z, y):
    size = buffers[0].shape[0] // 4
    for k, ref in enumerate(buffers):
        for i in range(4):
            at = pl.multiple_of(block_of(z, y, core, k, i) * rows, 16)
            start = i * size + first
            w[pl.ds(at, rows), :] = ref[start : start + rows, :]


def multiply_tokens(pieces, w, seq, store):
    own, below, above, far_top, far_bottom = pieces
    feats, half = own.shape[1], far_top.shape[0]

    def part(ref, step):
        at = pl.multiple_of(lax.rem(seq + step, NX) * feats, 128)
        return jnp.dot(ref[...], w[pl.ds(at, feats), :], preferred_element_type=F32)

    near = part(own, 0) + part(below, 3) + part(above, 1)
    store(slice(0, half), near[:half] + part(far_top, 2))
    store(slice(half, 2 * half), near[half:] + part(far_bottom, 2))


def kv_store(outs, core, gains):
    def store(rows, product):
        for out, group in zip(outs, GROUPS, strict=True):
            for n, h in enumerate(group):
                part = product[:, h * HD : (h + 1) * HD]
                out[rows, n * HD : (n + 1) * HD] = jnp.where(
                    core == 0, normed(part, gains[1:2, :]), part.astype(BF)
                )

    return store


def cross_kernel(gains, *refs):
    pieces, buffers = refs[:5], refs[5:13]
    outs, w = refs[13:-1], refs[-1]
    core, seq, z, y = place()
    assemble(w, buffers, 0, w.shape[0] // (NZ * NY), core, z, y)
    multiply_tokens(pieces, w, seq, kv_store(outs, core, gains))


def same_kernel(gains, *refs):
    pieces, w, outs = refs[:5], refs[5], refs[6:]
    core, seq, _, _ = place()
    multiply_tokens(pieces, w, seq, kv_store(outs, core, gains))


def pack_kernel(a, b, out):
    core = lax.axis_index("dp")
    size = a.shape[1]
    out[:, :size] = jnp.where(core == 0, a[...], b[...])
    out[:, size:] = jnp.where(core == 0, b[...], a[...])


def group_shapes(rows):
    return tuple(jax.ShapeDtypeStruct((rows, len(g) * HD), BF) for g in GROUPS)


def project_cross(gains, others, buffers):
    rows, feats = others[0].shape
    depth, width = NX * feats, buffers[0].shape[1]
    return call(
        cross_kernel,
        (*group_shapes(rows), jax.ShapeDtypeStruct((depth, width), BF)),
        (gains, *others, *buffers), [], 2 * rows * depth * width, 6 * 2**20, 20, "project_cross",
    )


def project_same(gains, tokens, w):
    rows, feats = tokens[0].shape
    depth, width = w.shape
    return call(
        same_kernel, group_shapes(rows), (gains, *tokens, w),
        [], 2 * rows * depth * width, 6 * 2**20, 20, "project_same",
    )


def half_kernel(first, *refs):
    buffers, w = refs[:8], refs[8]
    core, _, z, y = place()
    assemble(w, buffers, first, w.shape[0] // (NZ * NY), core, z, y)


def half_of(buffers, first, rows, name):
    width = buffers[0].shape[1]
    shape = jax.ShapeDtypeStruct((NZ * NY * rows, width), BF)
    return call(
        functools.partial(half_kernel, first), shape, buffers, [], 0, 2**22, 8, name
    )


def attend_frame(scale, q, key, value, keep):
    rows, keys = q.shape[0], key.shape[0]
    score = lax.dot_general(q, key, (((1,), (1,)), ((), ())), preferred_element_type=F32)
    weight = jnp.exp2(score * scale).reshape(rows // TILE, TILE, keys)
    weight = (weight * keep[:, None, :]).reshape(rows, keys).astype(BF)
    value = jnp.concatenate([value, jnp.ones((keys, HD), BF)], axis=1)
    return jnp.dot(weight, value, preferred_element_type=F32)


def picked(a, b, n):
    core = lax.axis_index("dp")
    at = slice(n * HD, (n + 1) * HD)
    return jnp.where(core == 0, a[:, at], b[:, at]), jnp.where(core == 0, b[:, at], a[:, at])


def unpacked(kv, n):
    size = kv.shape[1] // 2
    return kv[:, n * HD : (n + 1) * HD], kv[:, size + n * HD : size + (n + 1) * HD]


def kept(listed, frame, keys):
    tiles = listed.shape[0]
    lane = lax.div(lax.broadcasted_iota(jnp.int32, (tiles, keys), 1), TILE)
    tile = lane + frame * FRAME
    keep = jnp.zeros((tiles, keys), jnp.bool_)
    for s in range(listed.shape[1]):
        keep = keep | (tile == listed[:, s : s + 1])
    return jnp.where(keep & (tile >= 0), 1.0, 0.0)


def q_kernel(gains, w_own, w_other, *refs):
    pieces, q_ref, w = refs[:5], refs[5], refs[6]
    core, seq, _, _ = place()
    rows = w.shape[0] // (2 * NZ * NY)
    for block in range(NZ * NY):
        span = slice(block * rows, (block + 1) * rows)
        a, b = w_own[span, :], w_other[span, :]
        at = 2 * block * rows
        w[at : at + rows, :] = jnp.where(core == 0, a, b)
        w[at + rows : at + 2 * rows, :] = jnp.where(core == 0, b, a)

    def store(span, product):
        for h in range(product.shape[1] // HD):
            at = slice(h * HD, (h + 1) * HD)
            q_ref[span, at] = normed(product[:, at], gains[0:1, :])

    multiply_tokens(pieces, w, seq, store)


def own_kernel(scale, near, q_ref, *refs):
    acc = refs[-1]
    keep = kept(near[...], lax.axis_index("head"), q_ref.shape[0])
    for g, group in enumerate(GROUPS):
        for n, h in enumerate(group):
            key, value = picked(refs[2 * g], refs[2 * g + 1], n)
            acc[h] = attend_frame(scale, q_ref[:, h * HD : (h + 1) * HD], key, value, keep)


def attend_kernel(scale, group, near, q_ref, acc, *refs):
    sides, out = refs[:-1], refs[-1]
    head = lax.axis_index("head")
    keep = [kept(near[...], head + step, q_ref.shape[0]) for step in (-1, 1)]
    for n, h in enumerate(group):
        q = q_ref[:, h * HD : (h + 1) * HD]
        total = acc[h]
        for j in range(2):
            if len(sides) == 4:
                key, value = picked(sides[2 * j], sides[2 * j + 1], n)
            else:
                key, value = unpacked(sides[j], n)
            total = total + attend_frame(scale, q, key, value, keep[j])
        out[:, n * HD : (n + 1) * HD] = (total[:, :HD] / total[:, HD:]).astype(BF)


def output_kernel(group, w_own, w_other, total, *refs):
    pieces, out = refs[:-1], refs[-1]
    core, seq = lax.axis_index("dp"), lax.axis_index("seq")
    width, cols = w_own.shape[0] // NX, w_own.shape[1]
    size = len(group) * HD
    pairs = [
        (jnp.concatenate([pieces[i][...], pieces[j][...]], axis=1), (steps_i, steps_j))
        for (i, steps_i), (j, steps_j) in (((0, 0), (1, 3)), ((2, 1), (3, 2)))
    ]
    for w, side in ((w_own, core), (w_other, 1 - core)):
        to = pl.ds(pl.multiple_of(side * cols, HD), cols)
        product = None if total is None else total[:, to]
        for x, steps in pairs:
            rows = []
            for step in steps:
                at = pl.multiple_of(lax.rem(seq + step, NX) * width + group[0] * HD, HD)
                rows.append(w[pl.ds(at, size), :])
            part = jnp.dot(x, jnp.concatenate(rows, axis=0), preferred_element_type=F32)
            product = part if product is None else product + part
        out[:, to] = product.astype(out.dtype)


def first_kernel(group, w_own, w_other, *refs):
    output_kernel(group, w_own, w_other, None, *refs)


def direct_x(x):
    return x, along(x, "seq", 1), along(x, "seq", -1), along(x, "seq", 2)


def per_device(tokens_in, qkv_weight, norm_gains, out_weight, neighbours):
    rows, feats = tokens_in.shape
    width = qkv_weight.shape[2]
    heads = width // HD
    depth = qkv_weight.shape[0]
    mine = call(
        prepare_kernel,
        jax.ShapeDtypeStruct((depth * 3 // 2 + out_weight.shape[1], width), BF),
        (jnp.transpose(qkv_weight, (1, 0, 2)), jnp.transpose(out_weight)),
        [], 2**35, 2**20, 8, "prepare",
    )
    tokens, others, buffers = gathered(tokens_in, mine)

    w_q = half_of(buffers, depth, depth // 2, "query_half")
    w_q_other = swapped(w_q)
    *cross, w = project_cross(norm_gains, others, buffers)
    others_kv = [swapped(x) for x in cross]
    b0, b1 = (frames_on(cross[0], step, True) for step in (1, -1))
    gains, w, *others_kv = lax.optimization_barrier((norm_gains, w, *others_kv))
    same = project_same(gains, tokens, w)
    a0, a1 = (frames_on(same[0], step, False) for step in (1, -1))
    query = call(
        q_kernel, jax.ShapeDtypeStruct((rows, width), BF),
        (norm_gains, w_q, w_q_other, *tokens),
        [pltpu.VMEM((NX * feats, width), BF)], 2**35, 6 * 2**20, 20, "query",
    )
    late, _ = lax.optimization_barrier((same[1], query))
    packed = call(
        pack_kernel, jax.ShapeDtypeStruct((rows, 2 * late.shape[1]), BF),
        (late, others_kv[1]), [], 0, 2**19, 8, "pack",
    )
    sides = [(a0, b0, a1, b1), tuple(frames_on(packed, step, False) for step in (1, -1))]
    scale = HD ** (-0.5) * math.log2(math.e)
    acc = call(
        functools.partial(own_kernel, scale),
        jax.ShapeDtypeStruct((heads, rows, 2 * HD), F32),
        (neighbours, query, same[0], others_kv[0], same[1], others_kv[1]),
        [], 2**35, 6 * 2**20, 20, "own_frame",
    )
    first = depth * 3 // 2
    w_out = half_of(buffers, first, mine.shape[0] - first, "out_half")
    w_outs = (w_out, swapped(w_out))
    total = ()
    for g, group in enumerate(GROUPS):
        last = g == len(GROUPS) - 1
        out = call(
            functools.partial(attend_kernel, scale, group),
            jax.ShapeDtypeStruct((rows, len(group) * HD), BF),
            (neighbours, query, acc, *sides[g]),
            [], 2**30, 4 * 2**20, 16, "attend_%d" % g,
        )
        pieces = direct_x(out)
        total = (
            call(
                functools.partial(output_kernel if g else first_kernel, group),
                jax.ShapeDtypeStruct((rows, feats), BF if last else F32),
                (*w_outs, *total, *pieces),
                [], 8 * rows * feats * len(group) * HD, 5 * 2**20, 16, "output_%d" % g,
            ),
        )
    return total[0]


def solution(mesh):
    placed = (
        P(("dp", "head"), "seq"),
        P("head", None, "seq"),
        P(),
        P("seq", "head"),
        P(("dp", "head"), None),
    )
    return jax.shard_map(
        per_device, mesh=mesh, in_specs=placed, out_specs=P(("dp", "head"), "seq"), check_vma=False
    )
```
